128 devices in a mesh: board: 16 (over z, x_lo, core), hand: 8 (over y, x_hi).
Axes of the slice: x: 4 (x_hi: 2, x_lo: 2; x = x_hi * 2 + x_lo), y: 4, z: 4, core: 2. Of those that a mesh axis runs over, the one named last changes fastest.
Arguments:
- cum_turn: float32 [1408, 13, 8], P(('board', 'hand')), may hold values from 0.05 to 20
- cum_river: float32 [1408, 9, 13, 384], P(('board', 'hand')), may hold values from 0.05 to 20
- opp_init: float32 [1408, 8], P(('board', 'hand')), may hold values from 0.00021306818 to 0.0021306819
- turn_cards: int32 [8, 4], replicated, may hold values from 0 to 51, as said below
- strength: int32 [1408, 384], P(('board', 'hand')), may hold values from 0 to 255, as said below
Outputs:
- river_value: float32 [384, 9, 1408], P(('board', 'hand'))
- br_value: float32 [1408, 8], P(('board', 'hand'))
The draws below stay inside these ranges and needn't reach their ends.
Inputs may be any that keep to these rules, and one draw needn't show every extreme that they name: `turn_cards`: each row names four different cards. `strength`: on every river board some hand slot has level 0 and some has level 255.
All inputs are finite; a program needn't handle non-finite values.
Results may differ from the reference program's by a relative error of at most 0.0003.
Values may be sent and summed in bfloat16 or wider, within the bound.
No kernel may reach another device: no remote copies, remote signals or barrier semaphores. Data moves between devices by JAX's collectives and lax.ppermute only.
A program may use at most 128 MiB of HBM per device.

```python
import math
import jax
import jax.numpy as jnp
import numpy as np
from jax import lax

HANDS = 1408
LIVE = 1326
RIVERS = 48
BETS = 4
RANKS = 256
TURNS = 8
RBOARDS = 384
LINES = 9
OROWS = 13


def draw_turn_cards(key, part):
    key = jax.random.fold_in(key, 11)
    keys_all = jax.random.split(key, TURNS)
    return jax.vmap(lambda subkey: jax.random.permutation(subkey, 52)[:4])(keys_all).astype(jnp.int32)


def draw_strength(key, part):
    key = jax.random.fold_in(key, 23)
    first_key, second_key = jax.random.split(key)
    levels = jax.random.randint(first_key, (HANDS, RBOARDS), 0, RANKS)
    chosen = jax.random.randint(second_key, (1, RBOARDS), 0, HANDS)
    places = jnp.arange(HANDS)[:, None]
    levels = jnp.where(places == chosen, RANKS - 1, levels)
    levels = jnp.where(places == (chosen + 1) % HANDS, 0, levels)
    return levels.astype(jnp.int32)


def level_of(key, extent, cuts, smallest, largest):
    def one(dim, shards_of):
        heights = jax.random.uniform(jax.random.fold_in(jax.random.fold_in(key, 6), dim), (shards_of,), jnp.float32, smallest / len(cuts), largest / len(cuts))
        return jnp.repeat(jnp.exp(heights), extent[dim] // shards_of).reshape((-1,) + (1,) * (len(extent) - dim - 1))

    loudness = one(*cuts[0])
    for cut in cuts[1:]:
        loudness = loudness * one(*cut)
    return loudness


def setup_inputs(seed: int = 0) -> dict:
    key_list = jax.random.split(jax.random.key(seed), 6)
    return {
        "cum_turn": jnp.clip(jnp.exp(math.log(20.0) - 5.9914645 * jax.random.uniform(key_list[0], (HANDS, OROWS, TURNS), jnp.float32) ** level_of(key_list[0], (HANDS, OROWS, TURNS), ((0, 128),), -0.2, 0.2)), 0.05, 20.0),
        "cum_river": jnp.clip(jnp.exp(math.log(20.0) - 5.9914645 * jax.random.uniform(key_list[1], (HANDS, LINES, OROWS, RBOARDS), jnp.float32) ** level_of(key_list[1], (HANDS, LINES, OROWS, RBOARDS), ((0, 128),), -0.2, 0.2)), 0.05, 20.0),
        "opp_init": jnp.clip(jnp.exp(math.log(0.0021306819) - 2.3025851 * jax.random.uniform(key_list[2], (HANDS, TURNS), jnp.float32) ** level_of(key_list[2], (HANDS, TURNS), ((0, 128),), -0.2, 0.2)), 0.00021306818, 0.0021306819),
        "turn_cards": draw_turn_cards(jax.random.fold_in(key_list[5], 71), 0),
        "strength": draw_strength(jax.random.fold_in(key_list[5], 71), 0),
    }


pre_pot = 2.0


def grow_street(bet_cap):
    tree_nodes = []

    def add_leaf(leaf_kind, folder, put_zero, put_one):
        tree_nodes.append({"kind": leaf_kind, "player": -1, "folder": folder, "put": (put_zero, put_one), "children": []})
        return len(tree_nodes) - 1

    def grow_node(player, bet_count, put_zero, put_one):
        position = len(tree_nodes)
        tree_nodes.append({"kind": "act", "player": player, "folder": -1, "put": (put_zero, put_one), "children": []})
        own_put = put_zero if player == 0 else put_one
        rival_put = put_one if player == 0 else put_zero
        raised = rival_put + 1
        after_zero = raised if player == 0 else put_zero
        after_one = raised if player == 1 else put_one
        children = []
        if rival_put > own_put:
            children.append(add_leaf("fold", player, put_zero, put_one))
            children.append(add_leaf("end", -1, rival_put, rival_put))
        elif player == 0:
            children.append(grow_node(1, bet_count, put_zero, put_one))
        else:
            children.append(add_leaf("end", -1, put_zero, put_one))
        if bet_count < bet_cap:
            children.append(grow_node(1 - player, bet_count + 1, after_zero, after_one))
        tree_nodes[position]["children"] = children
        return position

    grow_node(0, 0, 0, 0)
    return tree_nodes


def street_tables(bet_cap):
    tree_nodes = grow_street(bet_cap)
    end_leaves = [node_id for node_id in range(len(tree_nodes)) if tree_nodes[node_id]["kind"] == "end"]
    fold_leaves = [node_id for node_id in range(len(tree_nodes)) if tree_nodes[node_id]["kind"] == "fold"]
    row_of = {}
    for node_id in range(len(tree_nodes)):
        if tree_nodes[node_id]["kind"] == "act" and tree_nodes[node_id]["player"] == 1:
            for child_id in tree_nodes[node_id]["children"]:
                row_of[child_id] = len(row_of)
    return tree_nodes, end_leaves, fold_leaves, row_of


def leaf_scales(tree_nodes, end_leaves, fold_leaves, line_puts):
    end_scale = np.zeros((len(line_puts), len(end_leaves)), np.float32)
    fold_scale = np.zeros((len(line_puts), len(fold_leaves)), np.float32)
    for line_id in range(len(line_puts)):
        for column, leaf_id in enumerate(end_leaves):
            end_scale[line_id, column] = pre_pot + line_puts[line_id][0] + tree_nodes[leaf_id]["put"][0]
        for column, leaf_id in enumerate(fold_leaves):
            folder = tree_nodes[leaf_id]["folder"]
            loser_put = pre_pot + line_puts[line_id][folder] + tree_nodes[leaf_id]["put"][folder]
            fold_scale[line_id, column] = loser_put if folder == 1 else -loser_put
    return end_scale, fold_scale


def hand_cards(hand_count):
    card_low = []
    card_high = []
    for low_card in range(52):
        for high_card in range(low_card + 1, 52):
            card_low.append(low_card)
            card_high.append(high_card)
    card_low = (card_low + [52] * hand_count)[:hand_count]
    card_high = (card_high + [53] * hand_count)[:hand_count]
    return np.array(card_low, np.int32), np.array(card_high, np.int32)


def make_shares(tree_nodes, row_of, picker):
    shares = {}
    for node_id in range(len(tree_nodes)):
        if tree_nodes[node_id]["kind"] == "act" and tree_nodes[node_id]["player"] == 1:
            children = tree_nodes[node_id]["children"]
            summed = picker(row_of[children[0]])
            for child_id in children[1:]:
                summed = summed + picker(row_of[child_id])
            for child_id in children:
                shares[child_id] = picker(row_of[child_id]) / summed
    return shares


def spread_reach(tree_nodes, shares, root_reach):
    reach_map = {0: root_reach}
    for node_id in range(len(tree_nodes)):
        if tree_nodes[node_id]["kind"] != "act":
            continue
        for child_id in tree_nodes[node_id]["children"]:
            if tree_nodes[node_id]["player"] == 1:
                reach_map[child_id] = reach_map[node_id] * shares[child_id]
            else:
                reach_map[child_id] = reach_map[node_id]
    return reach_map


def back_up(tree_nodes, leaf_values):
    values = dict(leaf_values)
    for node_id in reversed(range(len(tree_nodes))):
        if tree_nodes[node_id]["kind"] != "act":
            continue
        child_values = [values[child_id] for child_id in tree_nodes[node_id]["children"]]
        merged = child_values[0]
        for other_value in child_values[1:]:
            if tree_nodes[node_id]["player"] == 0:
                merged = jnp.maximum(merged, other_value)
            else:
                merged = merged + other_value
        values[node_id] = merged
    return values[0]


def board_values(hand_level, leaf_reach, apart_pairs, tree_parts):
    tree_nodes, end_leaves, fold_leaves, end_scale, fold_scale = tree_parts
    line_count = leaf_reach.shape[0]
    hand_count = leaf_reach.shape[2]
    ends_count = len(end_leaves)
    level_float = hand_level.astype(jnp.float32)
    living = level_float >= 0.0
    allowed = apart_pairs & living[:, None] & living[None, :]
    sign_matrix = jnp.where(allowed, jnp.sign(level_float[:, None] - level_float[None, :]), 0.0).astype(jnp.bfloat16)
    pair_mask = allowed.astype(jnp.bfloat16)
    end_rows = leaf_reach[:, :ends_count, :].reshape(-1, hand_count)
    fold_rows = leaf_reach[:, ends_count:, :].reshape(-1, hand_count)
    contract = (((1,), (1,)), ((), ()))
    showdown_sums = lax.dot_general(end_rows, sign_matrix, contract, preferred_element_type=jnp.float32).reshape(line_count, ends_count, hand_count)
    fold_sums = lax.dot_general(fold_rows, pair_mask, contract, preferred_element_type=jnp.float32).reshape(line_count, -1, hand_count)
    leaf_values = {}
    for column, leaf_id in enumerate(end_leaves):
        leaf_values[leaf_id] = showdown_sums[:, column, :] * end_scale[:, column][:, None]
    for column, leaf_id in enumerate(fold_leaves):
        leaf_values[leaf_id] = fold_sums[:, column, :] * fold_scale[:, column][:, None]
    return back_up(tree_nodes, leaf_values)


def reference(cum_turn, cum_river, opp_init, turn_cards, strength):
    tree_nodes, end_leaves, fold_leaves, row_of = street_tables(BETS)
    line_puts = [tree_nodes[leaf_id]["put"] for leaf_id in end_leaves]
    end_scale, fold_scale = leaf_scales(tree_nodes, end_leaves, fold_leaves, line_puts)
    unused_scale, turn_fold_scale = leaf_scales(tree_nodes, end_leaves, fold_leaves, [(0, 0)])
    tree_parts = (tree_nodes, end_leaves, fold_leaves, end_scale, fold_scale)
    low_table, high_table = hand_cards(HANDS)
    card_low = jnp.asarray(low_table)
    card_high = jnp.asarray(high_table)
    hand_ids = jnp.arange(HANDS, dtype=jnp.int32)
    deck_cards = jnp.arange(52, dtype=jnp.int32)
    in_turn = jnp.any(turn_cards[:, :, None] == deck_cards[None, None, :], axis=1)
    rest_rank = jnp.cumsum(jnp.where(in_turn, 0, 1).astype(jnp.int32), axis=1, dtype=jnp.int32) - 1
    picked = (rest_rank[:, None, :] == jnp.arange(RIVERS, dtype=jnp.int32)[None, :, None]) & jnp.logical_not(in_turn)[:, None, :]
    river_card = jnp.sum(jnp.where(picked, deck_cards[None, None, :], 0), axis=2, dtype=jnp.int32).reshape(RBOARDS)
    blocked = jnp.any((card_low[:, None, None] == turn_cards[None, :, :]) | (card_high[:, None, None] == turn_cards[None, :, :]), axis=2)
    alive_turn = (hand_ids < LIVE)[:, None] & jnp.logical_not(blocked)
    alive_river = jnp.repeat(alive_turn, RIVERS, axis=1) & (card_low[:, None] != river_card[None, :]) & (card_high[:, None] != river_card[None, :])
    apart_pairs = (card_low[:, None] != card_low[None, :]) & (card_low[:, None] != card_high[None, :]) & (card_high[:, None] != card_low[None, :]) & (card_high[:, None] != card_high[None, :])
    turn_shares = make_shares(tree_nodes, row_of, lambda row_id: cum_turn[:, row_id, :])
    turn_reach = spread_reach(tree_nodes, turn_shares, opp_init * alive_turn.astype(jnp.float32))
    line_reach = jnp.stack([turn_reach[leaf_id] for leaf_id in end_leaves], axis=1)
    fold_reach = jnp.stack([turn_reach[leaf_id] for leaf_id in fold_leaves], axis=1)
    hand_level = jnp.where(alive_river, strength, -1)

    def river_turn(turn_id):
        first_board = turn_id * RIVERS
        cum_here = lax.dynamic_slice_in_dim(cum_river, first_board, RIVERS, 3)
        living = lax.dynamic_slice_in_dim(alive_river, first_board, RIVERS, 1).astype(jnp.float32)
        root_reach = lax.dynamic_slice_in_dim(line_reach, turn_id, 1, 2) * living[:, None, :]
        shares = make_shares(tree_nodes, row_of, lambda row_id: cum_here[:, :, row_id, :])
        reach_map = spread_reach(tree_nodes, shares, root_reach)
        leaf_reach = jnp.stack([reach_map[leaf_id] for leaf_id in end_leaves + fold_leaves], axis=2).astype(jnp.bfloat16)
        levels_here = lax.dynamic_slice_in_dim(hand_level, first_board, RIVERS, 1)
        return lax.map(lambda pieces: board_values(pieces[0], pieces[1], apart_pairs, tree_parts), (jnp.transpose(levels_here), jnp.transpose(leaf_reach, (3, 1, 2, 0))))

    river_all = lax.map(river_turn, jnp.arange(TURNS, dtype=jnp.int32))
    river_value = river_all.reshape(RBOARDS, -1, HANDS)
    line_values = jnp.transpose(jnp.sum(river_all, axis=1), (2, 1, 0)) / RIVERS

    def turn_folds(turn_id):
        living = lax.dynamic_slice_in_dim(alive_turn, turn_id, 1, 1)[:, 0]
        allowed = (apart_pairs & living[:, None] & living[None, :]).astype(jnp.float32)
        reach_here = lax.dynamic_slice_in_dim(fold_reach, turn_id, 1, 2)[:, :, 0]
        return jnp.dot(allowed, reach_here, precision=lax.Precision.HIGHEST)

    fold_sums = jnp.transpose(lax.map(turn_folds, jnp.arange(TURNS, dtype=jnp.int32)), (1, 2, 0))
    leaf_values = {}
    for column, leaf_id in enumerate(end_leaves):
        leaf_values[leaf_id] = line_values[:, column, :]
    for column, leaf_id in enumerate(fold_leaves):
        leaf_values[leaf_id] = fold_sums[:, column, :] * turn_fold_scale[0, column]
    br_value = back_up(tree_nodes, leaf_values)
    return river_value, br_value
```

```python
import jax
import jax.numpy as jnp
import numpy as np
from jax import lax
from jax.experimental import pallas as pl
from jax.experimental.pallas import tpu as pltpu
from jax.sharding import PartitionSpec as P

LIVE = 1326
RIVERS = 48
BETS = 4
PRE_POT = 2.0
AXES = ("board", "hand")

HANDS = 1408
DEVICES = 128
OWNED = HANDS // DEVICES
LINES = 9
ROWS = 13
BOARDS = 384
TURNS = 8
LOCAL = BOARDS // DEVICES
SLOTS = 120
BOARD_SLOTS = OWNED * SLOTS
BLOCKS = 32
USED_BLOCKS = 31
LEVEL_SLOT = 117
VMEM = 56 * 1024 * 1024


def grow_street(bet_cap):
    tree_nodes = []

    def add_leaf(leaf_kind, folder, put_zero, put_one):
        tree_nodes.append(
            {
                "kind": leaf_kind,
                "player": -1,
                "folder": folder,
                "put": (put_zero, put_one),
                "children": [],
            }
        )
        return len(tree_nodes) - 1

    def grow_node(player, bet_count, put_zero, put_one):
        position = len(tree_nodes)
        tree_nodes.append(
            {
                "kind": "act",
                "player": player,
                "folder": -1,
                "put": (put_zero, put_one),
                "children": [],
            }
        )
        own_put = put_zero if player == 0 else put_one
        rival_put = put_one if player == 0 else put_zero
        raised = rival_put + 1
        after_zero = raised if player == 0 else put_zero
        after_one = raised if player == 1 else put_one
        children = []
        if rival_put > own_put:
            children.append(add_leaf("fold", player, put_zero, put_one))
            children.append(add_leaf("end", -1, rival_put, rival_put))
        elif player == 0:
            children.append(grow_node(1, bet_count, put_zero, put_one))
        else:
            children.append(add_leaf("end", -1, put_zero, put_one))
        if bet_count < bet_cap:
            children.append(grow_node(1 - player, bet_count + 1, after_zero, after_one))
        tree_nodes[position]["children"] = children
        return position

    grow_node(0, 0, 0, 0)
    return tree_nodes


TREE = grow_street(BETS)
ENDS = [i for i, node in enumerate(TREE) if node["kind"] == "end"]
FOLDS = [i for i, node in enumerate(TREE) if node["kind"] == "fold"]
ROW_OF = {}
for _i, _node in enumerate(TREE):
    if _node["kind"] == "act" and _node["player"] == 1:
        for _child in _node["children"]:
            ROW_OF[_child] = len(ROW_OF)
REACH_ROW = dict(ROW_OF)
for _i, _node in enumerate(TREE):
    if _node["kind"] == "act" and _node["player"] == 0 and _i > 0:
        for _child in _node["children"]:
            REACH_ROW[_child] = REACH_ROW[_i]
LINE_PUT = [TREE[i]["put"][0] for i in ENDS]


def hand_cards(hand_count):
    card_low = []
    card_high = []
    for low_card in range(52):
        for high_card in range(low_card + 1, 52):
            card_low.append(low_card)
            card_high.append(high_card)
    card_low = (card_low + [52] * hand_count)[:hand_count]
    card_high = (card_high + [53] * hand_count)[:hand_count]
    return np.array(card_low, np.int32), np.array(card_high, np.int32)


def back_up(leaf_values):
    values = dict(leaf_values)
    for node_id in reversed(range(len(TREE))):
        if TREE[node_id]["kind"] != "act":
            continue
        child_values = [values[child_id] for child_id in TREE[node_id]["children"]]
        merged = child_values[0]
        for other_value in child_values[1:]:
            if TREE[node_id]["player"] == 0:
                merged = jnp.maximum(merged, other_value)
            else:
                merged = merged + other_value
        values[node_id] = merged
    return values[0]


def node_rows():
    nodes = []
    for i, node in enumerate(TREE):
        if node["kind"] == "act" and node["player"] == 1:
            parent = REACH_ROW.get(i, -1)
            nodes.append((parent, [ROW_OF[c] for c in node["children"]]))
    return nodes


def sort_four(cards):
    a, b, c, d = cards
    a, b = jnp.minimum(a, b), jnp.maximum(a, b)
    c, d = jnp.minimum(c, d), jnp.maximum(c, d)
    a, c = jnp.minimum(a, c), jnp.maximum(a, c)
    b, d = jnp.minimum(b, d), jnp.maximum(b, d)
    b, c = jnp.minimum(b, c), jnp.maximum(b, c)
    return a, b, c, d


def river_from(cards, rank):
    river = rank
    for card in sort_four(cards):
        river = river + jnp.where(river >= card, 1, 0)
    return river


def device_index():
    return lax.axis_index("board") * lax.axis_size("hand") + lax.axis_index("hand")


def send_kernel(
    turn_cards, cum_turn, opp_init, strength, cum_river, out, cum, turn_rows, root, reach, wide, sems
):
    def fetch(k):
        return pltpu.make_async_copy(cum_river.at[k], cum.at[k], sems.at[k])

    for k in range(OWNED):
        fetch(k).start()
    f32 = jnp.float32
    first_hand = device_index() * OWNED
    hand = first_hand + lax.broadcasted_iota(jnp.int32, (16, 1), 0)
    low = jnp.zeros((16, 1), jnp.int32)
    for card in range(1, 52):
        low = low + jnp.where(hand >= card * (103 - card) // 2, 1, 0)
    high = hand - ((low * (103 - low)) >> 1) + low + 1
    board = lax.broadcasted_iota(jnp.int32, (1, BOARDS), 1)
    turn = jnp.zeros((1, BOARDS), jnp.int32)
    for q in range(1, TURNS):
        turn = turn + jnp.where(board >= RIVERS * q, 1, 0)
    cards = []
    for c in range(4):
        card = jnp.zeros((1, BOARDS), jnp.int32)
        for t in range(TURNS):
            card = jnp.where(turn == t, turn_cards[t, c], card)
        cards.append(card)
    river = river_from(cards, board - RIVERS * turn)
    free = hand < LIVE
    for card in cards:
        free = free & (low != card) & (high != card)
    alive_turn = jnp.where(free, 1.0, 0.0).astype(f32)
    alive = jnp.where(free & (low != river) & (high != river), 1.0, 0.0).astype(f32)

    turn_rows[...] = jnp.zeros(turn_rows.shape, f32)
    start = opp_init[...]
    reach_map = {-1: start}
    for parent, rows in node_rows():
        picked = [cum_turn[:, row, :] for row in rows]
        summed = picked[0]
        for other in picked[1:]:
            summed = summed + other
        for row, value in zip(rows, picked):
            reach_map[row] = reach_map[parent] * (value / summed)
            turn_rows[16 * row : 16 * row + OWNED, 0:TURNS] = reach_map[row]
    lane_turn = lax.broadcasted_iota(jnp.int32, (128, BOARDS), 0)
    spread = jnp.where(lane_turn == turn, 1.0, 0.0).astype(f32)
    spread_rows = lax.dot_general(
        turn_rows[...],
        spread,
        (((1,), (0,)), ((), ())),
        precision=lax.Precision.HIGHEST,
        preferred_element_type=f32,
    )
    for line, leaf in enumerate(ENDS):
        row = REACH_ROW[leaf]
        root[line] = spread_rows[16 * row : 16 * row + 16] * alive
    owner = (board * 171) >> 9
    fold_pick = owner & 7
    folded = jnp.zeros((16, BOARDS), f32)
    for f, leaf in enumerate(FOLDS):
        row = REACH_ROW[leaf]
        folded = jnp.where(fold_pick == f, spread_rows[16 * row : 16 * row + 16], folded)
    folded = folded * alive_turn
    fold_head = folded.astype(jnp.bfloat16).astype(f32)
    fold_tail = folded - fold_head
    level = strength[...].astype(f32)
    for k in range(OWNED):
        base = k * SLOTS + LEVEL_SLOT
        reach[base : base + 1, :] = level[k : k + 1]
        reach[base + 1 : base + 2, :] = fold_head[k : k + 1]
        reach[base + 2 : base + 3, :] = fold_tail[k : k + 1]

    row_head = lax.broadcasted_iota(jnp.int32, (8, 1), 0)
    row_tail = lax.broadcasted_iota(jnp.int32, (5, 1), 0) + 8
    nodes = node_rows()

    def spread_over(row_ids, parts):
        merged = parts[-1]
        for (_, rows), part in reversed(list(zip(nodes[:-1], parts[:-1]))):
            merged = jnp.where(row_ids <= rows[-1], part, merged)
        return merged

    for k in range(OWNED):
        fetch(k).wait()
        for line in range(LINES):
            x_head = cum[k, line, 0:8, :]
            x_tail = cum[k, line, 8:13, :]
            rows = [cum[k, line, r : r + 1, :] for r in range(ROWS)]
            sums = []
            for _, ids in nodes:
                summed = rows[ids[0]]
                for r in ids[1:]:
                    summed = summed + rows[r]
                sums.append(summed)
            start = root[line, k : k + 1, :]
            q_head = x_head / spread_over(row_head, sums)
            q_tail = x_tail / spread_over(row_tail, sums)
            at_bet = start * q_head[1:2]
            at_raise = at_bet * q_head[4:5]
            at_reraise = start * q_tail[1:2]
            parents = [start, at_bet, at_raise, start, at_reraise]
            base = k * SLOTS
            reach[base + 8 * line : base + 8 * line + 8, :] = q_head * spread_over(
                row_head, parents
            )
            reach[base + 72 + 5 * line : base + 77 + 5 * line, :] = q_tail * spread_over(
                row_tail, parents
            )

    dest = lax.broadcasted_iota(jnp.int32, (DEVICES, BOARDS), 0)
    lane = lax.broadcasted_iota(jnp.int32, (DEVICES, BOARDS), 1)
    picks = [
        jnp.where(lane == LOCAL * dest + b, 1.0, 0.0).astype(jnp.bfloat16) for b in range(LOCAL)
    ]
    block_lane = lax.broadcasted_iota(jnp.int32, (DEVICES, 128), 1)

    def pick(b, values):
        return lax.dot_general(
            picks[b],
            values.astype(jnp.bfloat16),
            (((1,), (1,)), ((), ())),
            preferred_element_type=f32,
        )

    for m in range(USED_BLOCKS):
        first = 128 * m
        b = first // BOARD_SLOTS
        inside = first - b * BOARD_SLOTS
        room = min(128, BOARD_SLOTS - inside)
        part = reach[inside : inside + room, :]
        if room == 128:
            block = pick(b, part)
        elif b == LOCAL - 1:
            block = pick(b, jnp.concatenate([part, jnp.zeros((128 - room, BOARDS), f32)], 0))
        else:
            both = jnp.concatenate([part, reach[0 : 128 - room, :]], 0)
            block = jnp.where(block_lane < room, pick(b, both), pick(b + 1, both))
        wide[pl.ds(m, DEVICES, stride=BLOCKS), :] = block
    for m in range(USED_BLOCKS, BLOCKS):
        wide[pl.ds(m, DEVICES, stride=BLOCKS), :] = jnp.zeros((DEVICES, 128), f32)
    out[...] = wide[...].astype(jnp.bfloat16)


def send(turn_cards, cum_turn, opp_init, strength, cum_river):
    vmem = pl.BlockSpec(memory_space=pltpu.VMEM)
    return pl.pallas_call(
        send_kernel,
        in_specs=[
            pl.BlockSpec(memory_space=pltpu.SMEM),
            vmem,
            vmem,
            vmem,
            pl.BlockSpec(memory_space=pl.ANY),
        ],
        out_specs=vmem,
        out_shape=jax.ShapeDtypeStruct((DEVICES * BLOCKS, 128), jnp.bfloat16),
        scratch_shapes=[
            pltpu.VMEM((OWNED, LINES, ROWS, BOARDS), jnp.float32),
            pltpu.VMEM((16 * ROWS, 128), jnp.float32),
            pltpu.VMEM((LINES, 16, BOARDS), jnp.float32),
            pltpu.VMEM((BOARD_SLOTS, BOARDS), jnp.float32),
            pltpu.VMEM((DEVICES * BLOCKS, 128), jnp.float32),
            pltpu.SemaphoreType.DMA((OWNED,)),
        ],
        compiler_params=pltpu.CompilerParams(vmem_limit_bytes=VMEM),
        name="send_reach",
    )(turn_cards, cum_turn, opp_init, strength, cum_river)


def apart_kernel(marks, out):
    shared = lax.dot_general(
        marks[...], marks[...], (((1,), (1,)), ((), ())), preferred_element_type=jnp.float32
    )
    out[...] = jnp.where(shared == 0.0, 1.0, 0.0).astype(jnp.bfloat16)


def make_apart(marks):
    vmem = pl.BlockSpec(memory_space=pltpu.VMEM)
    return pl.pallas_call(
        apart_kernel,
        in_specs=[vmem],
        out_specs=vmem,
        out_shape=jax.ShapeDtypeStruct((HANDS, HANDS), jnp.bfloat16),
        compiler_params=pltpu.CompilerParams(vmem_limit_bytes=VMEM),
        name="apart_pairs",
    )(marks)


def stake_column(rows):
    line = lax.broadcasted_iota(jnp.int32, (rows, 1), 0)
    stake = jnp.zeros((rows, 1), jnp.float32)
    for i in range(rows):
        stake = jnp.where(line == i, PRE_POT + LINE_PUT[i], stake)
    return stake


def street_values(stake, end_sum, fold_sum):
    leaf_values = {}
    for leaf in ENDS:
        leaf_values[leaf] = end_sum(REACH_ROW[leaf]) * (stake + TREE[leaf]["put"][0])
    for leaf in FOLDS:
        folder = TREE[leaf]["folder"]
        lost = stake + TREE[leaf]["put"][folder]
        leaf_values[leaf] = fold_sum(REACH_ROW[leaf]) * (lost if folder == 1 else -lost)
    return back_up(leaf_values)


def board_kernel(
    turn_cards, cards, recv, apart_hbm, river_out, sums_out, apart, wide, turned, lhs, folds, marks, sem
):
    f32 = jnp.float32
    fetch = pltpu.make_async_copy(apart_hbm, apart, sem)
    fetch.start()
    wide[...] = recv[...].astype(f32)
    for m in range(USED_BLOCKS):
        block = wide[pl.ds(m, DEVICES, stride=BLOCKS), :]
        turned[128 * m : 128 * m + 128, :] = block.T
    for b in range(LOCAL):
        for k in range(OWNED):
            base = SLOTS * (OWNED * b + k)
            parts = [turned[pl.ds(base + r, 8, stride=8), :] for r in range(8)]
            parts += [turned[pl.ds(base + 72 + r, 8, stride=5), :] for r in range(5)]
            parts.append(turned[base + 64 : base + 72, :])
            parts.append(turned[base + 112 : base + 120, :])
            parts.append(jnp.zeros((8, 128), f32))
            lhs[128 * b : 128 * b + 128, 128 * k : 128 * k + 128] = jnp.concatenate(
                parts, 0
            ).astype(jnp.bfloat16)
    fetch.wait()
    folds[...] = jnp.dot(lhs[...], apart[...], preferred_element_type=f32)

    first_board = device_index() * LOCAL
    turn = first_board // RIVERS
    board_cards = [turn_cards[turn, c] for c in range(4)]
    low = cards[0:1, :]
    high = cards[1:2, :]
    free = low < 52
    for card in board_cards:
        free = free & (low != card) & (high != card)
    alive_turn = jnp.where(free, 1.0, 0.0).astype(f32)
    stake = stake_column(8)
    last_stake = PRE_POT + LINE_PUT[8]
    total = jnp.zeros((8, HANDS), f32)
    last_total = jnp.zeros((1, HANDS), f32)
    for b in range(LOCAL):
        river = river_from(board_cards, first_board + b - turn * RIVERS)
        alive = jnp.where(free & (low != river) & (high != river), 1.0, 0.0).astype(f32)
        rows = [
            turned[SLOTS * (OWNED * b + k) + LEVEL_SLOT : SLOTS * (OWNED * b + k) + LEVEL_SLOT + 1, :]
            for k in range(OWNED)
        ]
        level_row = jnp.concatenate(rows, 1).astype(jnp.bfloat16)
        signs = []
        for k in range(OWNED):
            u = SLOTS * (OWNED * b + k) + LEVEL_SLOT
            block = wide[pl.ds(u // 128, DEVICES, stride=BLOCKS), :]
            column = block[:, u % 128 : u % 128 + 1]
            column = jnp.broadcast_to(column, (DEVICES, 128)).astype(jnp.bfloat16)
            column = jnp.concatenate([column] * OWNED, 1)
            sign = jnp.clip(level_row - column, -1.0, 1.0)
            signs.append(sign * apart[128 * k : 128 * k + 128, :])
        sign = jnp.concatenate(signs, 0)
        ends = jnp.dot(lhs[128 * b : 128 * b + 128, :], sign, preferred_element_type=f32)
        values = street_values(
            stake,
            lambda r: ends[8 * r : 8 * r + 8],
            lambda r: folds[128 * b + 8 * r : 128 * b + 8 * r + 8, :],
        )
        last = street_values(
            last_stake,
            lambda r: ends[104 + r : 105 + r],
            lambda r: folds[128 * b + 104 + r : 128 * b + 105 + r, :],
        )
        values = values * alive
        last = last * alive
        river_out[b, 0:8, :] = values
        river_out[b, 8:9, :] = last
        total = total + values
        last_total = last_total + last
    fold_total = (folds[118:119, :] + folds[119:120, :]) * alive_turn
    marks[...] = jnp.zeros((128, 128), f32)
    for k in range(OWNED):
        lanes = slice(128 * k, 128 * k + 128)
        marks[8 * k : 8 * k + 8, :] = total[:, lanes]
        marks[88 + k : 89 + k, :] = last_total[:, lanes]
        marks[99 + k : 100 + k, :] = fold_total[:, lanes]
    sums_out[...] = marks[...].T


def boards(turn_cards, cards, recv, apart):
    vmem = pl.BlockSpec(memory_space=pltpu.VMEM)
    return pl.pallas_call(
        board_kernel,
        in_specs=[
            pl.BlockSpec(memory_space=pltpu.SMEM),
            vmem,
            vmem,
            pl.BlockSpec(memory_space=pl.ANY),
        ],
        out_specs=(vmem, vmem),
        out_shape=(
            jax.ShapeDtypeStruct((LOCAL, LINES, HANDS), jnp.float32),
            jax.ShapeDtypeStruct((DEVICES, 128), jnp.float32),
        ),
        scratch_shapes=[
            pltpu.VMEM((HANDS, HANDS), jnp.bfloat16),
            pltpu.VMEM((DEVICES * BLOCKS, 128), jnp.float32),
            pltpu.VMEM((DEVICES * BLOCKS, 128), jnp.float32),
            pltpu.VMEM((LOCAL * 128, HANDS), jnp.bfloat16),
            pltpu.VMEM((LOCAL * 128, HANDS), jnp.float32),
            pltpu.VMEM((128, 128), jnp.float32),
            pltpu.SemaphoreType.DMA,
        ],
        compiler_params=pltpu.CompilerParams(vmem_limit_bytes=VMEM),
        name="board_values",
    )(turn_cards, cards, recv, apart)


def turn_kernel(recv, out, turned):
    group = DEVICES // TURNS
    line_sum = jnp.zeros((TURNS, 128), jnp.float32)
    for g in range(group):
        line_sum = line_sum + recv[pl.ds(g, TURNS, stride=group), :]
    parts = [line_sum]
    for f in range(len(FOLDS)):
        parts.append(recv[pl.ds(f, TURNS, stride=group), :])
    parts.append(jnp.zeros((128 - 8 * len(parts), 128), jnp.float32))
    turned[...] = jnp.concatenate(parts, 0).T
    leaf_values = {}
    for line, leaf in enumerate(ENDS):
        if line < 8:
            value = turned[pl.ds(line, OWNED, stride=8), :]
        else:
            value = turned[88 : 88 + OWNED, :]
        leaf_values[leaf] = value[:, 0:TURNS] / float(RIVERS)
    folds = turned[99 : 99 + OWNED, :]
    for f, leaf in enumerate(FOLDS):
        folder = TREE[leaf]["folder"]
        lost = PRE_POT + TREE[leaf]["put"][folder]
        leaf_values[leaf] = folds[:, 8 * f + 8 : 8 * f + 16] * (lost if folder == 1 else -lost)
    out[...] = back_up(leaf_values)


def turns(recv):
    vmem = pl.BlockSpec(memory_space=pltpu.VMEM)
    return pl.pallas_call(
        turn_kernel,
        in_specs=[vmem],
        out_specs=vmem,
        out_shape=jax.ShapeDtypeStruct((OWNED, TURNS), jnp.float32),
        scratch_shapes=[pltpu.VMEM((128, 128), jnp.float32)],
        name="turn_values",
    )(recv)


def body(cum_turn, cum_river, opp_init, turn_cards, strength):
    low, high = hand_cards(HANDS)
    order = np.arange(HANDS).reshape(DEVICES, OWNED).T.reshape(-1)
    low, high = low[order], high[order]
    cards = np.zeros((8, HANDS), np.int32)
    cards[0], cards[1] = low, high
    deck = np.arange(128)
    marks = ((low[:, None] == deck) | (high[:, None] == deck)).astype(np.float32)

    packed = send(turn_cards, cum_turn, opp_init, strength, cum_river)
    packed = packed.reshape(DEVICES, BLOCKS, 128)
    recv = lax.all_to_all(packed, AXES, split_axis=0, concat_axis=0, tiled=True)
    apart = make_apart(jnp.asarray(marks, jnp.bfloat16))
    river, sums = boards(
        turn_cards, jnp.asarray(cards), recv.reshape(DEVICES * BLOCKS, 128), apart
    )
    back = lax.all_to_all(
        sums.reshape(DEVICES, 1, 128), AXES, split_axis=0, concat_axis=0, tiled=True
    )
    river = river.reshape(LOCAL, LINES, OWNED, DEVICES)
    river_value = jnp.transpose(river, (0, 1, 3, 2)).reshape(LOCAL, LINES, HANDS)
    return river_value, turns(back.reshape(DEVICES, 128))


def solution(mesh):
    placed = (
        P(AXES, None, None),
        P(AXES, None, None, None),
        P(AXES, None),
        P(),
        P(AXES, None),
    )
    return jax.shard_map(
        body,
        mesh=mesh,
        in_specs=placed,
        out_specs=(P(AXES, None, None), P(AXES, None)),
        check_vma=False,
    )
```

```python
import jax
import jax.numpy as jnp
import numpy as np
from jax import lax
from jax.experimental import pallas as pl
from jax.experimental.pallas import tpu as pltpu
from jax.sharding import PartitionSpec as P

LIVE = 1326
RIVERS = 48
BETS = 4
PRE_POT = 2.0
UNROLL = True
AXES = ("board", "hand")

HANDS = 1408
DEVICES = 128
OWNED = HANDS // DEVICES
LINES = 9
ROWS = 13
BOARDS = 384
TURNS = 8
LOCAL = BOARDS // DEVICES
SLOTS = 88
BOARD_SLOTS = OWNED * SLOTS
BLOCKS = 24
USED_BLOCKS = 23
PITCH = 24
BOARD_ROWS = 96
LEVEL_SLOT = 81
VMEM = 48 * 1024 * 1024


def grow_street(bet_cap):
    tree_nodes = []

    def add_leaf(leaf_kind, folder, put_zero, put_one):
        tree_nodes.append(
            {
                "kind": leaf_kind,
                "player": -1,
                "folder": folder,
                "put": (put_zero, put_one),
                "children": [],
            }
        )
        return len(tree_nodes) - 1

    def grow_node(player, bet_count, put_zero, put_one):
        position = len(tree_nodes)
        tree_nodes.append(
            {
                "kind": "act",
                "player": player,
                "folder": -1,
                "put": (put_zero, put_one),
                "children": [],
            }
        )
        own_put = put_zero if player == 0 else put_one
        rival_put = put_one if player == 0 else put_zero
        raised = rival_put + 1
        after_zero = raised if player == 0 else put_zero
        after_one = raised if player == 1 else put_one
        children = []
        if rival_put > own_put:
            children.append(add_leaf("fold", player, put_zero, put_one))
            children.append(add_leaf("end", -1, rival_put, rival_put))
        elif player == 0:
            children.append(grow_node(1, bet_count, put_zero, put_one))
        else:
            children.append(add_leaf("end", -1, put_zero, put_one))
        if bet_count < bet_cap:
            children.append(grow_node(1 - player, bet_count + 1, after_zero, after_one))
        tree_nodes[position]["children"] = children
        return position

    grow_node(0, 0, 0, 0)
    return tree_nodes


TREE = grow_street(BETS)
ENDS = [i for i, node in enumerate(TREE) if node["kind"] == "end"]
FOLDS = [i for i, node in enumerate(TREE) if node["kind"] == "fold"]
ROW_OF = {}
for _i, _node in enumerate(TREE):
    if _node["kind"] == "act" and _node["player"] == 1:
        for _child in _node["children"]:
            ROW_OF[_child] = len(ROW_OF)
REACH_ROW = dict(ROW_OF)
for _i, _node in enumerate(TREE):
    if _node["kind"] == "act" and _node["player"] == 0 and _i > 0:
        for _child in _node["children"]:
            REACH_ROW[_child] = REACH_ROW[_i]
LINE_PUT = [TREE[i]["put"][0] for i in ENDS]

SENT = [10, 11, 2, 3, 8, 5, 6, 7, 12]
SUM_OF = {4: ([5, 6], []), 9: ([10, 11, 12], []), 1: ([2, 3, 4], []), 0: ([7, 8, 9], [1])}


def hand_cards(hand_count):
    card_low = []
    card_high = []
    for low_card in range(52):
        for high_card in range(low_card + 1, 52):
            card_low.append(low_card)
            card_high.append(high_card)
    card_low = (card_low + [52] * hand_count)[:hand_count]
    card_high = (card_high + [53] * hand_count)[:hand_count]
    return np.array(card_low, np.int32), np.array(card_high, np.int32)


def back_up(leaf_values):
    values = dict(leaf_values)
    for node_id in reversed(range(len(TREE))):
        if TREE[node_id]["kind"] != "act":
            continue
        child_values = [values[child_id] for child_id in TREE[node_id]["children"]]
        merged = child_values[0]
        for other_value in child_values[1:]:
            if TREE[node_id]["player"] == 0:
                merged = jnp.maximum(merged, other_value)
            else:
                merged = merged + other_value
        values[node_id] = merged
    return values[0]


def node_rows():
    nodes = []
    for i, node in enumerate(TREE):
        if node["kind"] == "act" and node["player"] == 1:
            parent = REACH_ROW.get(i, -1)
            nodes.append((parent, [ROW_OF[c] for c in node["children"]]))
    return nodes


def sort_four(cards):
    a, b, c, d = cards
    a, b = jnp.minimum(a, b), jnp.maximum(a, b)
    c, d = jnp.minimum(c, d), jnp.maximum(c, d)
    a, c = jnp.minimum(a, c), jnp.maximum(a, c)
    b, d = jnp.minimum(b, d), jnp.maximum(b, d)
    b, c = jnp.minimum(b, c), jnp.maximum(b, c)
    return a, b, c, d


def river_from(cards, rank):
    river = rank
    for card in sort_four(cards):
        river = river + jnp.where(river >= card, 1, 0)
    return river


def device_index():
    return lax.axis_index("board") * lax.axis_size("hand") + lax.axis_index("hand")


def send_kernel(
    turn_cards, cum_turn, opp_init, strength, cum_river, out, cum, turn_rows, root, reach, wide, sems
):
    def fetch(k):
        return pltpu.make_async_copy(cum_river.at[k], cum.at[k], sems.at[k])

    for k in range(OWNED):
        fetch(k).start()
    f32 = jnp.float32
    first_hand = device_index() * OWNED
    hand = first_hand + lax.broadcasted_iota(jnp.int32, (16, 1), 0)
    low = jnp.zeros((16, 1), jnp.int32)
    for card in range(1, 52):
        low = low + jnp.where(hand >= card * (103 - card) // 2, 1, 0)
    high = hand - ((low * (103 - low)) >> 1) + low + 1
    board = lax.broadcasted_iota(jnp.int32, (1, BOARDS), 1)
    turn = jnp.zeros((1, BOARDS), jnp.int32)
    for q in range(1, TURNS):
        turn = turn + jnp.where(board >= RIVERS * q, 1, 0)
    cards = []
    for c in range(4):
        card = jnp.zeros((1, BOARDS), jnp.int32)
        for t in range(TURNS):
            card = jnp.where(turn == t, turn_cards[c, t], card)
        cards.append(card)
    river = river_from(cards, board - RIVERS * turn)
    free = hand < LIVE
    for card in cards:
        free = free & (low != card) & (high != card)
    alive_turn = jnp.where(free, 1.0, 0.0).astype(f32)
    alive = jnp.where(free & (low != river) & (high != river), 1.0, 0.0).astype(f32)

    turn_rows[...] = jnp.zeros(turn_rows.shape, f32)
    turn_rows[0 : OWNED * TURNS, 0:ROWS] = cum_turn[...].reshape(OWNED * TURNS, ROWS)
    turn_rows[128 : 128 + TURNS, 0:OWNED] = opp_init[...]
    by_row = turn_rows[0:128, :].T
    start = turn_rows[128:256, :].T[0:16]
    reach_map = {-1: None}
    lane = lax.broadcasted_iota(jnp.int32, (16, 128), 1)
    own = (lane >> 3) == lax.broadcasted_iota(jnp.int32, (16, 128), 0)
    stacked = [start]
    for parent, rows in node_rows():
        picked = [by_row[row : row + 1] for row in rows]
        summed = picked[0]
        for other in picked[1:]:
            summed = summed + other
        for row, value in zip(rows, picked):
            share = value / summed
            reach_map[row] = share if parent < 0 else reach_map[parent] * share
    for row in range(ROWS):
        stacked.append(jnp.where(own, reach_map[row], 0.0))
    lane_turn = lax.broadcasted_iota(jnp.int32, (128, BOARDS), 0)
    spread = jnp.where((lane_turn & 7) == turn, 1.0, 0.0).astype(f32)
    spread = jnp.where(lane_turn < OWNED * TURNS, spread, 0.0)
    spread_all = lax.dot_general(
        jnp.concatenate(stacked, 0),
        spread,
        (((1,), (0,)), ((), ())),
        precision=lax.Precision.HIGHEST,
        preferred_element_type=f32,
    )
    opponent = spread_all[0:16]
    alive_turn = alive_turn * opponent
    alive = alive * opponent
    spread_rows = spread_all[16:]
    for line, leaf in enumerate(ENDS):
        row = REACH_ROW[leaf]
        root[line] = spread_rows[16 * row : 16 * row + 16] * alive
    owner = (board * 171) >> 9
    fold_pick = owner & 7
    folded = jnp.zeros((16, BOARDS), f32)
    for f, leaf in enumerate(FOLDS):
        row = REACH_ROW[leaf]
        folded = jnp.where(fold_pick == f, spread_rows[16 * row : 16 * row + 16], folded)
    folded = folded * alive_turn
    fold_head = folded.astype(jnp.bfloat16).astype(f32)
    fold_tail = folded - fold_head
    level = strength[...].astype(f32)
    for k in range(OWNED):
        reach[k, 80:88, :] = jnp.zeros((8, BOARDS), f32)
        reach[k, 81:82, :] = level[k : k + 1]
        reach[k, 82:83, :] = fold_head[k : k + 1]
        reach[k, 83:84, :] = fold_tail[k : k + 1]

    row_head = lax.broadcasted_iota(jnp.int32, (8, 1), 0)
    row_tail = lax.broadcasted_iota(jnp.int32, (8, 1), 0) + 8
    nodes = node_rows()

    def spread_over(row_ids, parts):
        merged = parts[-1]
        for (_, rows), part in reversed(list(zip(nodes[:-1], parts[:-1]))):
            merged = jnp.where(row_ids <= rows[-1], part, merged)
        return merged

    def one_hand(k, carry):
        fetch(k).wait()
        for line in range(LINES):
            x_head = cum[k, line, 0:8, :]
            x_tail = jnp.concatenate([cum[k, line, 8:13, :], jnp.ones((3, BOARDS), f32)], 0)
            rows = [cum[k, line, r : r + 1, :] for r in range(ROWS)]
            sums = []
            for _, ids in nodes:
                summed = rows[ids[0]]
                for r in ids[1:]:
                    summed = summed + rows[r]
                sums.append(summed)
            start = root[line, pl.ds(k, 1), :]
            q_head = x_head / spread_over(row_head, sums)
            q_tail = x_tail / spread_over(row_tail, sums)
            at_bet = start * q_head[1:2]
            at_raise = at_bet * q_head[4:5]
            at_reraise = start * q_tail[1:2]
            parents = [start, at_bet, at_raise, start, at_reraise]
            head = q_head * spread_over(row_head, parents)
            tail = q_tail * spread_over(row_tail, parents)
            mixed = jnp.where(
                row_head < 2,
                pltpu.roll(tail, 6, 0),
                jnp.where(row_head == 4, pltpu.roll(tail, 4, 0), head),
            )
            reach[k, 8 * line : 8 * line + 8, :] = mixed
            reach[k, 72 + line : 73 + line, :] = tail[4:5]
        return carry

    lax.fori_loop(0, OWNED, one_hand, 0, unroll=True)

    dest = lax.broadcasted_iota(jnp.int32, (DEVICES, BOARDS), 0)
    lane = lax.broadcasted_iota(jnp.int32, (DEVICES, BOARDS), 1)
    picks = [
        jnp.where(lane == LOCAL * dest + b, 1.0, 0.0).astype(jnp.bfloat16) for b in range(LOCAL)
    ]
    block_lane = lax.broadcasted_iota(jnp.int32, (DEVICES, 128), 1)

    def pick(b, values):
        return lax.dot_general(
            picks[b],
            values.astype(jnp.bfloat16),
            (((1,), (1,)), ((), ())),
            preferred_element_type=f32,
        )

    flat = reach.reshape(BOARD_SLOTS, BOARDS)

    def put(m, block):
        wide.reshape(DEVICES * PITCH, 128)[pl.ds(m, DEVICES, stride=PITCH), :] = block

    for b in range(LOCAL):
        first = -(-b * BOARD_SLOTS // 128)
        last = (b + 1) * BOARD_SLOTS // 128

        def whole_block(m, carry):
            start = pl.multiple_of(128 * m - b * BOARD_SLOTS, 8)
            put(m, pick(b, flat[pl.ds(start, 128), :]))
            return carry

        lax.fori_loop(first, last, whole_block, 0, unroll=UNROLL)
        inside = 128 * last - b * BOARD_SLOTS
        room = BOARD_SLOTS - inside
        part = flat[inside:BOARD_SLOTS, :]
        if b == LOCAL - 1:
            put(last, pick(b, jnp.concatenate([part, jnp.zeros((128 - room, BOARDS), f32)], 0)))
        else:
            both = jnp.concatenate([part, flat[0 : 128 - room, :]], 0)
            put(last, jnp.where(block_lane < room, pick(b, both), pick(b + 1, both)))
    for m in range(USED_BLOCKS, BLOCKS):
        put(m, jnp.zeros((DEVICES, 128), f32))
    out[...] = wide[:, 0:BLOCKS, :].astype(jnp.bfloat16).reshape(DEVICES * BLOCKS, 128)


def keep(space, *arrays):
    return [pltpu.with_memory_space_constraint(array, space) for array in arrays]


def send(turn_cards, cum_turn, opp_init, strength, cum_river):
    vmem = pl.BlockSpec(memory_space=pltpu.VMEM)
    turn_cards, cum_turn, opp_init, strength, cum_river = keep(
        pltpu.HBM, turn_cards, cum_turn, opp_init, strength, cum_river
    )
    return pl.pallas_call(
        send_kernel,
        in_specs=[
            pl.BlockSpec(memory_space=pltpu.SMEM),
            vmem,
            vmem,
            vmem,
            pl.BlockSpec(memory_space=pl.ANY),
        ],
        out_specs=vmem,
        out_shape=pltpu.VMEM((DEVICES * BLOCKS, 128), jnp.bfloat16),
        scratch_shapes=[
            pltpu.VMEM((OWNED, LINES, ROWS, BOARDS), jnp.float32),
            pltpu.VMEM((256, 128), jnp.float32),
            pltpu.VMEM((LINES, 16, BOARDS), jnp.float32),
            pltpu.VMEM((OWNED, SLOTS, BOARDS), jnp.float32),
            pltpu.VMEM((DEVICES, PITCH, 128), jnp.float32),
            pltpu.SemaphoreType.DMA((OWNED,)),
        ],
        compiler_params=pltpu.CompilerParams(vmem_limit_bytes=VMEM),
        name="send_reach",
    )(turn_cards, cum_turn, opp_init, strength, cum_river)


def apart_kernel(marks, out):
    shared = lax.dot_general(
        marks[...], marks[...], (((1,), (1,)), ((), ())), preferred_element_type=jnp.float32
    )
    out[...] = jnp.where(shared == 0.0, 1.0, 0.0).astype(jnp.bfloat16)


def make_apart(marks):
    vmem = pl.BlockSpec(memory_space=pltpu.VMEM)
    (marks,) = keep(pltpu.HBM, marks)
    return pl.pallas_call(
        apart_kernel,
        in_specs=[vmem],
        out_specs=vmem,
        out_shape=pltpu.HBM((HANDS, HANDS), jnp.bfloat16),
        compiler_params=pltpu.CompilerParams(vmem_limit_bytes=VMEM),
        name="apart_pairs",
    )(marks)


def stake_column(rows):
    line = lax.broadcasted_iota(jnp.int32, (rows, 1), 0)
    stake = jnp.zeros((rows, 1), jnp.float32)
    for i in range(rows):
        stake = jnp.where(line == i, PRE_POT + LINE_PUT[i], stake)
    return stake


def all_rows(sums):
    sums = dict(sums)
    for row, (plus, minus) in SUM_OF.items():
        total = sums[plus[0]]
        for other in plus[1:]:
            total = total + sums[other]
        for other in minus:
            total = total - sums[other]
        sums[row] = total
    return sums


def street_values(stake, end_sums, fold_sums):
    end_sums = all_rows(end_sums)
    fold_sums = all_rows(fold_sums)
    leaf_values = {}
    for leaf in ENDS:
        leaf_values[leaf] = end_sums[REACH_ROW[leaf]] * (stake + TREE[leaf]["put"][0])
    for leaf in FOLDS:
        folder = TREE[leaf]["folder"]
        lost = stake + TREE[leaf]["put"][folder]
        leaf_values[leaf] = fold_sums[REACH_ROW[leaf]] * (lost if folder == 1 else -lost)
    return back_up(leaf_values)


def board_kernel(
    turn_cards,
    cards,
    recv,
    apart_hbm,
    marks_in_hbm,
    marks_out_hbm,
    river_out,
    sums_out,
    apart,
    marks_in,
    marks_out,
    wide,
    turned,
    lhs,
    columns,
    ends,
    folds,
    marks,
    sems,
):
    f32 = jnp.float32
    bf16 = jnp.bfloat16
    loads = [
        pltpu.make_async_copy(marks_in_hbm, marks_in, sems.at[0]),
        pltpu.make_async_copy(marks_out_hbm, marks_out, sems.at[1]),
        pltpu.make_async_copy(apart_hbm, apart, sems.at[2]),
    ]
    for load in loads:
        load.start()
    wide[:, 0:BLOCKS, :] = recv[...].astype(f32).reshape(DEVICES, BLOCKS, 128)

    def turn_block(m, carry):
        block = wide.reshape(DEVICES * PITCH, 128)[pl.ds(m, DEVICES, stride=PITCH), :]
        turned[pl.ds(pl.multiple_of(128 * m, 128), 128), :] = block.T
        return carry

    lax.fori_loop(0, USED_BLOCKS, turn_block, 0, unroll=UNROLL)

    for b in range(LOCAL):

        def one_hand(k, carry):
            base = pl.multiple_of(SLOTS * (OWNED * b + k), 8)
            lanes = pl.ds(pl.multiple_of(128 * k, 128), 128)
            parts = [turned[pl.ds(base + g, 8, stride=8), :] for g in range(8)]
            for first in (72, 64, 80):
                parts.append(turned[pl.ds(base + first, 8), :])
            parts.append(jnp.zeros((8, 128), f32))
            lhs[BOARD_ROWS * b : BOARD_ROWS * (b + 1), lanes] = jnp.concatenate(parts, 0).astype(
                bf16
            )
            return carry

        lax.fori_loop(0, OWNED, one_hand, 0, unroll=UNROLL)

    level_rows = jnp.concatenate(
        [
            turned[pl.ds(LEVEL_SLOT, LOCAL * OWNED, stride=SLOTS), :],
            jnp.zeros((128 - LOCAL * OWNED, 128), f32),
        ],
        0,
    )
    level_columns = level_rows.T
    for q in range(LOCAL * OWNED):
        column = level_columns[:, q : q + 1]
        columns[q] = jnp.broadcast_to(column, (DEVICES, 128)).astype(bf16)

    loads[0].wait()
    loads[1].wait()
    card_sums = jnp.dot(lhs[...], marks_in[...], preferred_element_type=f32)
    lane = lax.broadcasted_iota(jnp.int32, card_sums.shape, 1)
    head = card_sums.astype(bf16).astype(f32)
    middle = (card_sums - head).astype(bf16).astype(f32)
    tail = card_sums - head - middle
    split = jnp.where(lane < 64, head, jnp.where(lane < 128, middle, tail)).astype(bf16)
    folds[...] = jnp.dot(split, marks_out[...], preferred_element_type=f32) + lhs[...].astype(f32)
    loads[2].wait()

    first_board = device_index() * LOCAL
    turn = first_board // RIVERS
    board_cards = [turn_cards[c, turn] for c in range(4)]
    low = cards[0:1, :]
    high = cards[1:2, :]
    free = low < 52
    for card in board_cards:
        free = free & (low != card) & (high != card)
    alive_turn = jnp.where(free, 1.0, 0.0).astype(f32)
    stake = stake_column(8)
    last_stake = PRE_POT + LINE_PUT[8]
    total = jnp.zeros((8, HANDS), f32)
    last_total = jnp.zeros((1, HANDS), f32)
    for b in range(LOCAL):
        river = river_from(board_cards, first_board + b - turn * RIVERS)
        alive = jnp.where(free & (low != river) & (high != river), 1.0, 0.0).astype(f32)
        row_tiles = [
            jnp.concatenate(
                [jnp.broadcast_to(level_rows[OWNED * b + k : OWNED * b + k + 1], (16, 128))] * 8, 0
            ).astype(bf16)
            for k in range(OWNED)
        ]
        rows = slice(BOARD_ROWS * b, BOARD_ROWS * (b + 1))
        for first in range(0, OWNED, 2):
            tiles = range(first, min(first + 2, OWNED))
            lanes = slice(128 * first, 128 * (tiles[-1] + 1))
            signs = []
            for k in range(OWNED):
                column = columns[OWNED * b + k]
                pieces = []
                for i in tiles:
                    pair = apart[128 * k : 128 * k + 128, 128 * i : 128 * i + 128]
                    pieces.append(jnp.clip(row_tiles[i] - column, -1.0, 1.0) * pair)
                signs.append(jnp.concatenate(pieces, 1))
            sign = jnp.concatenate(signs, 0)
            ends[rows, lanes] = jnp.dot(lhs[rows, :], sign, preferred_element_type=f32)
        base = BOARD_ROWS * b

        def main_rows(sums):
            return {
                r: sums[base + 8 * i : base + 8 * i + 8, :] for i, r in enumerate(SENT)
            }

        def last_rows(sums):
            return {r: sums[base + 72 + i : base + 73 + i, :] for i, r in enumerate(SENT)}

        values = street_values(stake, main_rows(ends), main_rows(folds))
        last = street_values(last_stake, last_rows(ends), last_rows(folds))
        values = values * alive
        last = last * alive
        river_out[b, 0:8, :] = values
        river_out[b, 8:9, :] = last
        total = total + values
        last_total = last_total + last
    fold_total = (folds[82:83, :] + folds[83:84, :]) * alive_turn
    marks[...] = jnp.zeros((128, 128), f32)
    for k in range(OWNED):
        lanes = slice(128 * k, 128 * k + 128)
        marks[8 * k : 8 * k + 8, :] = total[:, lanes]
        marks[88 + k : 89 + k, :] = last_total[:, lanes]
        marks[99 + k : 100 + k, :] = fold_total[:, lanes]
    sums_out[...] = marks[...].T


def boards(turn_cards, cards, recv, apart, marks_in, marks_out):
    vmem = pl.BlockSpec(memory_space=pltpu.VMEM)
    hbm = pl.BlockSpec(memory_space=pl.ANY)
    (recv,) = keep(pltpu.VMEM, recv)
    turn_cards, cards, apart, marks_in, marks_out = keep(
        pltpu.HBM, turn_cards, cards, apart, marks_in, marks_out
    )
    return pl.pallas_call(
        board_kernel,
        in_specs=[pl.BlockSpec(memory_space=pltpu.SMEM), vmem, vmem, hbm, hbm, hbm],
        out_specs=(vmem, vmem),
        out_shape=(
            jax.ShapeDtypeStruct((LOCAL, LINES, HANDS), jnp.float32),
            pltpu.VMEM((DEVICES, 128), jnp.float32),
        ),
        scratch_shapes=[
            pltpu.VMEM((HANDS, HANDS), jnp.bfloat16),
            pltpu.VMEM((HANDS, 256), jnp.bfloat16),
            pltpu.VMEM((256, HANDS), jnp.bfloat16),
            pltpu.VMEM((DEVICES, PITCH, 128), jnp.float32),
            pltpu.VMEM((DEVICES * BLOCKS, 128), jnp.float32),
            pltpu.VMEM((LOCAL * BOARD_ROWS, HANDS), jnp.bfloat16),
            pltpu.VMEM((LOCAL * OWNED, DEVICES, 128), jnp.bfloat16),
            pltpu.VMEM((LOCAL * BOARD_ROWS, HANDS), jnp.float32),
            pltpu.VMEM((LOCAL * BOARD_ROWS, HANDS), jnp.float32),
            pltpu.VMEM((128, 128), jnp.float32),
            pltpu.SemaphoreType.DMA((3,)),
        ],
        compiler_params=pltpu.CompilerParams(vmem_limit_bytes=VMEM),
        name="board_values",
    )(turn_cards, cards, recv, apart, marks_in, marks_out)


def turn_kernel(recv, out, turned, best):
    group = DEVICES // TURNS
    line_sum = jnp.zeros((TURNS, 128), jnp.float32)
    for g in range(group):
        line_sum = line_sum + recv[pl.ds(g, TURNS, stride=group), :]
    parts = [line_sum]
    for f in range(len(FOLDS)):
        parts.append(recv[pl.ds(f, TURNS, stride=group), :])
    parts.append(jnp.zeros((128 - 8 * len(parts), 128), jnp.float32))
    turned[...] = jnp.concatenate(parts, 0).T
    leaf_values = {}
    for line, leaf in enumerate(ENDS):
        if line < 8:
            value = turned[pl.ds(line, OWNED, stride=8), :]
        else:
            value = turned[88 : 88 + OWNED, :]
        leaf_values[leaf] = value[:, 0:TURNS] / float(RIVERS)
    folds = turned[99 : 99 + OWNED, :]
    for f, leaf in enumerate(FOLDS):
        folder = TREE[leaf]["folder"]
        lost = PRE_POT + TREE[leaf]["put"][folder]
        leaf_values[leaf] = folds[:, 8 * f + 8 : 8 * f + 16] * (lost if folder == 1 else -lost)
    best[0:OWNED, 0:TURNS] = back_up(leaf_values)
    out[...] = best[...].T[0:TURNS, 0:OWNED]


def turns(recv):
    vmem = pl.BlockSpec(memory_space=pltpu.VMEM)
    (recv,) = keep(pltpu.VMEM, recv)
    return pl.pallas_call(
        turn_kernel,
        in_specs=[vmem],
        out_specs=vmem,
        out_shape=jax.ShapeDtypeStruct((TURNS, OWNED), jnp.float32),
        scratch_shapes=[pltpu.VMEM((128, 128), jnp.float32), pltpu.VMEM((128, 128), jnp.float32)],
        name="turn_values",
    )(recv)


def body(cum_turn, cum_river, opp_init, turn_cards, strength):
    low, high = hand_cards(HANDS)
    order = np.arange(HANDS).reshape(DEVICES, OWNED).T.reshape(-1)
    low, high = low[order], high[order]
    cards = np.zeros((8, HANDS), np.int32)
    cards[0], cards[1] = low, high
    deck = np.arange(128)
    marks = ((low[:, None] == deck) | (high[:, None] == deck)).astype(np.float32)
    marks_in = np.zeros((HANDS, 256), np.float32)
    marks_out = np.zeros((256, HANDS), np.float32)
    for copy in range(3):
        marks_in[:, 64 * copy : 64 * copy + 64] = marks[:, 0:64]
        marks_out[64 * copy : 64 * copy + 52] = 0.5 - marks.T[0:52]

    turn_cards = turn_cards.T
    packed = send(
        turn_cards, jnp.transpose(cum_turn, (0, 2, 1)), opp_init.T, strength, cum_river
    )
    packed = packed.reshape(DEVICES, BLOCKS, 128)
    recv = lax.all_to_all(packed, AXES, split_axis=0, concat_axis=0, tiled=True)
    apart = make_apart(jnp.asarray(marks, jnp.bfloat16))
    river, sums = boards(
        turn_cards,
        jnp.asarray(cards),
        recv.reshape(DEVICES * BLOCKS, 128),
        apart,
        jnp.asarray(marks_in, jnp.bfloat16),
        jnp.asarray(marks_out, jnp.bfloat16),
    )
    back = lax.all_to_all(
        sums.reshape(DEVICES, 1, 128), AXES, split_axis=0, concat_axis=0, tiled=True
    )
    river = river.reshape(LOCAL, LINES, OWNED, DEVICES)
    river_value = jnp.transpose(river, (0, 1, 3, 2)).reshape(LOCAL, LINES, HANDS)
    return river_value, turns(back.reshape(DEVICES, 128)).T


def solution(mesh):
    placed = (
        P(AXES, None, None),
        P(AXES, None, None, None),
        P(AXES, None),
        P(),
        P(AXES, None),
    )
    return jax.shard_map(
        body,
        mesh=mesh,
        in_specs=placed,
        out_specs=(P(AXES, None, None), P(AXES, None)),
        check_vma=False,
    )
```

```python
import jax
import jax.numpy as jnp
import numpy as np
from jax import lax
from jax.experimental import pallas as pl
from jax.experimental.pallas import tpu as pltpu
from jax.sharding import PartitionSpec as P

LIVE = 1326
RIVERS = 48
BETS = 4
PRE_POT = 2.0
UNROLL = True
GROUP = 3
AXES = ("board", "hand")

HANDS = 1408
DEVICES = 128
OWNED = HANDS // DEVICES
LINES = 9
ROWS = 13
BOARDS = 384
TURNS = 8
LOCAL = BOARDS // DEVICES
SLOTS = 88
BOARD_SLOTS = OWNED * SLOTS
BLOCKS = 24
BOARD_BLOCKS = BLOCKS // LOCAL
CHUNK = 256
CHUNKS = -(-HANDS // CHUNK)
PITCH = 24
BOARD_ROWS = 96
LEVEL_SLOT = 81
VMEM = 32 * 1024 * 1024


def grow_street(bet_cap):
    tree_nodes = []

    def add_leaf(leaf_kind, folder, put_zero, put_one):
        tree_nodes.append(
            {
                "kind": leaf_kind,
                "player": -1,
                "folder": folder,
                "put": (put_zero, put_one),
                "children": [],
            }
        )
        return len(tree_nodes) - 1

    def grow_node(player, bet_count, put_zero, put_one):
        position = len(tree_nodes)
        tree_nodes.append(
            {
                "kind": "act",
                "player": player,
                "folder": -1,
                "put": (put_zero, put_one),
                "children": [],
            }
        )
        own_put = put_zero if player == 0 else put_one
        rival_put = put_one if player == 0 else put_zero
        raised = rival_put + 1
        after_zero = raised if player == 0 else put_zero
        after_one = raised if player == 1 else put_one
        children = []
        if rival_put > own_put:
            children.append(add_leaf("fold", player, put_zero, put_one))
            children.append(add_leaf("end", -1, rival_put, rival_put))
        elif player == 0:
            children.append(grow_node(1, bet_count, put_zero, put_one))
        else:
            children.append(add_leaf("end", -1, put_zero, put_one))
        if bet_count < bet_cap:
            children.append(grow_node(1 - player, bet_count + 1, after_zero, after_one))
        tree_nodes[position]["children"] = children
        return position

    grow_node(0, 0, 0, 0)
    return tree_nodes


TREE = grow_street(BETS)
ENDS = [i for i, node in enumerate(TREE) if node["kind"] == "end"]
FOLDS = [i for i, node in enumerate(TREE) if node["kind"] == "fold"]
ROW_OF = {}
for _i, _node in enumerate(TREE):
    if _node["kind"] == "act" and _node["player"] == 1:
        for _child in _node["children"]:
            ROW_OF[_child] = len(ROW_OF)
REACH_ROW = dict(ROW_OF)
for _i, _node in enumerate(TREE):
    if _node["kind"] == "act" and _node["player"] == 0 and _i > 0:
        for _child in _node["children"]:
            REACH_ROW[_child] = REACH_ROW[_i]
LINE_PUT = [TREE[i]["put"][0] for i in ENDS]

SENT = [10, 11, 2, 3, 8, 5, 6, 7, 12]
SUM_OF = {4: ([5, 6], []), 9: ([10, 11, 12], []), 1: ([2, 3, 4], []), 0: ([7, 8, 9], [1])}


def hand_cards(hand_count):
    card_low = []
    card_high = []
    for low_card in range(52):
        for high_card in range(low_card + 1, 52):
            card_low.append(low_card)
            card_high.append(high_card)
    card_low = (card_low + [52] * hand_count)[:hand_count]
    card_high = (card_high + [53] * hand_count)[:hand_count]
    return np.array(card_low, np.int32), np.array(card_high, np.int32)


def back_up(leaf_values):
    values = dict(leaf_values)
    for node_id in reversed(range(len(TREE))):
        if TREE[node_id]["kind"] != "act":
            continue
        child_values = [values[child_id] for child_id in TREE[node_id]["children"]]
        merged = child_values[0]
        for other_value in child_values[1:]:
            if TREE[node_id]["player"] == 0:
                merged = jnp.maximum(merged, other_value)
            else:
                merged = merged + other_value
        values[node_id] = merged
    return values[0]


def node_rows():
    nodes = []
    for i, node in enumerate(TREE):
        if node["kind"] == "act" and node["player"] == 1:
            parent = REACH_ROW.get(i, -1)
            nodes.append((parent, [ROW_OF[c] for c in node["children"]]))
    return nodes


def sort_four(cards):
    a, b, c, d = cards
    a, b = jnp.minimum(a, b), jnp.maximum(a, b)
    c, d = jnp.minimum(c, d), jnp.maximum(c, d)
    a, c = jnp.minimum(a, c), jnp.maximum(a, c)
    b, d = jnp.minimum(b, d), jnp.maximum(b, d)
    b, c = jnp.minimum(b, c), jnp.maximum(b, c)
    return a, b, c, d


def river_from(cards, rank):
    river = rank
    for card in sort_four(cards):
        river = river + jnp.where(river >= card, 1, 0)
    return river


def device_index():
    return lax.axis_index("board") * lax.axis_size("hand") + lax.axis_index("hand")


def send_kernel(
    turn_cards_hbm,
    cum_turn_hbm,
    opp_init_hbm,
    strength_hbm,
    cum_river,
    out,
    turn_cards,
    cum_turn,
    opp_init,
    strength,
    cum,
    turn_rows,
    root,
    reach,
    by_board,
    wide,
    sems,
):
    loads = [
        pltpu.make_async_copy(source, target, sems.at[i])
        for i, (source, target) in enumerate(
            [
                (cum_turn_hbm, cum_turn),
                (opp_init_hbm, opp_init),
                (turn_cards_hbm, turn_cards),
                (strength_hbm, strength),
            ]
        )
    ]
    fetches = []
    for i, first in enumerate(range(0, OWNED, GROUP)):
        part = pl.ds(first, min(GROUP, OWNED - first))
        fetches.append(
            pltpu.make_async_copy(cum_river.at[part], cum.at[part], sems.at[len(loads) + i])
        )
    for copy in loads + fetches:
        copy.start()
    f32 = jnp.float32
    first_hand = device_index() * OWNED
    hand = first_hand + lax.broadcasted_iota(jnp.int32, (16, 1), 0)
    low = jnp.zeros((16, 1), jnp.int32)
    for card in range(1, 52):
        low = low + jnp.where(hand >= card * (103 - card) // 2, 1, 0)
    high = hand - ((low * (103 - low)) >> 1) + low + 1
    board = lax.broadcasted_iota(jnp.int32, (1, BOARDS), 1)
    turn = jnp.zeros((1, BOARDS), jnp.int32)
    for q in range(1, TURNS):
        turn = turn + jnp.where(board >= RIVERS * q, 1, 0)
    loads[2].wait()
    cards = []
    for c in range(4):
        card = jnp.zeros((1, BOARDS), jnp.int32)
        for t in range(TURNS):
            card = jnp.where(turn == t, turn_cards[c, t], card)
        cards.append(card)
    river = river_from(cards, board - RIVERS * turn)
    free = hand < LIVE
    for card in cards:
        free = free & (low != card) & (high != card)
    alive_turn = jnp.where(free, 1.0, 0.0).astype(f32)
    alive = jnp.where(free & (low != river) & (high != river), 1.0, 0.0).astype(f32)

    turn_rows[...] = jnp.zeros(turn_rows.shape, f32)
    loads[0].wait()
    loads[1].wait()
    turn_rows[0 : OWNED * TURNS, 0:ROWS] = cum_turn[...].reshape(OWNED * TURNS, ROWS)
    turn_rows[128 : 128 + TURNS, 0:OWNED] = opp_init[...]
    by_row = turn_rows[0:128, :].T
    start = turn_rows[128:256, :].T[0:16]
    reach_map = {-1: None}
    lane = lax.broadcasted_iota(jnp.int32, (16, 128), 1)
    own = (lane >> 3) == lax.broadcasted_iota(jnp.int32, (16, 128), 0)
    stacked = [start]
    for parent, rows in node_rows():
        picked = [by_row[row : row + 1] for row in rows]
        summed = picked[0]
        for other in picked[1:]:
            summed = summed + other
        for row, value in zip(rows, picked):
            share = value / summed
            reach_map[row] = share if parent < 0 else reach_map[parent] * share
    for row in range(ROWS):
        stacked.append(jnp.where(own, reach_map[row], 0.0))
    lane_turn = lax.broadcasted_iota(jnp.int32, (128, BOARDS), 0)
    spread = jnp.where((lane_turn & 7) == turn, 1.0, 0.0).astype(f32)
    spread = jnp.where(lane_turn < OWNED * TURNS, spread, 0.0)
    spread_all = lax.dot_general(
        jnp.concatenate(stacked, 0),
        spread,
        (((1,), (0,)), ((), ())),
        precision=lax.Precision.HIGHEST,
        preferred_element_type=f32,
    )
    opponent = spread_all[0:16]
    alive_turn = alive_turn * opponent
    alive = alive * opponent
    spread_rows = spread_all[16:]
    for line, leaf in enumerate(ENDS):
        row = REACH_ROW[leaf]
        root[line] = spread_rows[16 * row : 16 * row + 16] * alive
    owner = (board * 171) >> 9
    fold_pick = owner & 7
    folded = jnp.zeros((16, BOARDS), f32)
    for f, leaf in enumerate(FOLDS):
        row = REACH_ROW[leaf]
        folded = jnp.where(fold_pick == f, spread_rows[16 * row : 16 * row + 16], folded)
    folded = folded * alive_turn
    fold_head = folded.astype(jnp.bfloat16).astype(f32)
    fold_tail = folded - fold_head
    loads[3].wait()
    level = strength[...].astype(f32)
    for k in range(OWNED):
        base = SLOTS * k
        reach[base + 80 : base + 88, :] = jnp.zeros((8, BOARDS), f32)
        reach[base + 81 : base + 82, :] = level[k : k + 1]
        reach[base + 82 : base + 83, :] = fold_head[k : k + 1]
        reach[base + 83 : base + 84, :] = fold_tail[k : k + 1]
    reach[BOARD_SLOTS:, :] = jnp.zeros((128 * BOARD_BLOCKS - BOARD_SLOTS, BOARDS), f32)

    row_head = lax.broadcasted_iota(jnp.int32, (8, 1), 0)
    row_tail = lax.broadcasted_iota(jnp.int32, (8, 1), 0) + 8
    nodes = node_rows()

    def spread_over(row_ids, parts):
        merged = parts[-1]
        for (_, rows), part in reversed(list(zip(nodes[:-1], parts[:-1]))):
            merged = jnp.where(row_ids <= rows[-1], part, merged)
        return merged

    def one_hand(k):
        for line in range(LINES):
            x_head = cum[k, line, 0:8, :]
            x_tail = jnp.concatenate([cum[k, line, 8:13, :], jnp.ones((3, BOARDS), f32)], 0)
            rows = [cum[k, line, r : r + 1, :] for r in range(ROWS)]
            sums = []
            for _, ids in nodes:
                summed = rows[ids[0]]
                for r in ids[1:]:
                    summed = summed + rows[r]
                sums.append(summed)
            start = root[line, pl.ds(k, 1), :]
            q_head = x_head / spread_over(row_head, sums)
            q_tail = x_tail / spread_over(row_tail, sums)
            at_bet = start * q_head[1:2]
            at_raise = at_bet * q_head[4:5]
            at_reraise = start * q_tail[1:2]
            parents = [start, at_bet, at_raise, start, at_reraise]
            head = q_head * spread_over(row_head, parents)
            tail = q_tail * spread_over(row_tail, parents)
            mixed = jnp.where(
                row_head < 2,
                pltpu.roll(tail, 6, 0),
                jnp.where(row_head == 4, pltpu.roll(tail, 4, 0), head),
            )
            base = SLOTS * k
            reach[base + 8 * line : base + 8 * line + 8, :] = mixed
            reach[base + 72 + line : base + 73 + line, :] = tail[4:5]

    for k in range(OWNED):
        if k % GROUP == 0:
            fetches[k // GROUP].wait()
        one_hand(k)

    flat_wide = wide.reshape(DEVICES * PITCH, 128)
    for j in range(BOARD_BLOCKS):
        for i in range(LOCAL):
            by_board[j, 128 * i : 128 * i + 128, :] = reach[
                128 * j : 128 * j + 128, 128 * i : 128 * i + 128
            ].T
        for b in range(LOCAL):
            flat_wide[pl.ds(BOARD_BLOCKS * b + j, DEVICES, stride=PITCH), :] = by_board[
                j, pl.ds(b, DEVICES, stride=LOCAL), :
            ]
    out[...] = wide[:, 0:BLOCKS, :].astype(jnp.bfloat16).reshape(DEVICES * BLOCKS, 128)


def keep(space, *arrays):
    return [pltpu.with_memory_space_constraint(array, space) for array in arrays]


def send(turn_cards, cum_turn, opp_init, strength, cum_river):
    args = keep(pltpu.HBM, turn_cards, cum_turn, opp_init, strength, cum_river)
    return pl.pallas_call(
        send_kernel,
        in_specs=[pl.BlockSpec(memory_space=pl.ANY)] * len(args),
        out_specs=pl.BlockSpec(memory_space=pltpu.VMEM),
        out_shape=pltpu.VMEM((DEVICES * BLOCKS, 128), jnp.bfloat16),
        scratch_shapes=[
            pltpu.SMEM(turn_cards.shape, jnp.int32),
            pltpu.VMEM(cum_turn.shape, jnp.float32),
            pltpu.VMEM(opp_init.shape, jnp.float32),
            pltpu.VMEM(strength.shape, jnp.int32),
            pltpu.VMEM((OWNED, LINES, ROWS, BOARDS), jnp.float32),
            pltpu.VMEM((256, 128), jnp.float32),
            pltpu.VMEM((LINES, 16, BOARDS), jnp.float32),
            pltpu.VMEM((128 * BOARD_BLOCKS, BOARDS), jnp.float32),
            pltpu.VMEM((BOARD_BLOCKS, BOARDS, 128), jnp.float32),
            pltpu.VMEM((DEVICES, PITCH, 128), jnp.float32),
            pltpu.SemaphoreType.DMA((4 + -(-OWNED // GROUP),)),
        ],
        compiler_params=pltpu.CompilerParams(vmem_limit_bytes=VMEM),
        name="send_reach",
    )(*args)


def stake_column(rows):
    line = lax.broadcasted_iota(jnp.int32, (rows, 1), 0)
    stake = jnp.zeros((rows, 1), jnp.float32)
    for i in range(rows):
        stake = jnp.where(line == i, PRE_POT + LINE_PUT[i], stake)
    return stake


def all_rows(sums):
    sums = dict(sums)
    for row, (plus, minus) in SUM_OF.items():
        total = sums[plus[0]]
        for other in plus[1:]:
            total = total + sums[other]
        for other in minus:
            total = total - sums[other]
        sums[row] = total
    return sums


def street_values(stake, end_sums, fold_sums):
    end_sums = all_rows(end_sums)
    fold_sums = all_rows(fold_sums)
    leaf_values = {}
    for leaf in ENDS:
        leaf_values[leaf] = end_sums[REACH_ROW[leaf]] * (stake + TREE[leaf]["put"][0])
    for leaf in FOLDS:
        folder = TREE[leaf]["folder"]
        lost = stake + TREE[leaf]["put"][folder]
        leaf_values[leaf] = fold_sums[REACH_ROW[leaf]] * (lost if folder == 1 else -lost)
    return back_up(leaf_values)


def board_kernel(
    turn_cards_hbm,
    cards,
    recv,
    pairs,
    river_out,
    sums_out,
    turn_cards,
    wide,
    turned,
    lhs,
    columns,
    ends,
    folds,
    marks,
    sems,
):
    f32 = jnp.float32
    bf16 = jnp.bfloat16
    card_load = pltpu.make_async_copy(turn_cards_hbm, turn_cards, sems.at[0])
    card_load.start()
    wide[:, 0:BLOCKS, :] = recv[...].astype(f32).reshape(DEVICES, BLOCKS, 128)
    for m in range(BLOCKS):
        block = wide.reshape(DEVICES * PITCH, 128)[pl.ds(m, DEVICES, stride=PITCH), :]
        turned[128 * m : 128 * m + 128, :] = block.T
    for b in range(LOCAL):
        for k in range(OWNED):
            base = 128 * BOARD_BLOCKS * b + SLOTS * k
            parts = [turned[pl.ds(base + g, 8, stride=8), :] for g in range(8)]
            for first in (72, 64, 80):
                parts.append(turned[pl.ds(base + first, 8), :])
            parts.append(jnp.zeros((8, 128), f32))
            lhs[BOARD_ROWS * b : BOARD_ROWS * (b + 1), 128 * k : 128 * k + 128] = jnp.concatenate(
                parts, 0
            ).astype(bf16)

    def fold_sums(rows):
        card_marks = pairs[HANDS : HANDS + 256, :]
        card_sums = lax.dot_general(
            lhs[rows, :], card_marks, (((1,), (1,)), ((), ())), preferred_element_type=f32
        )
        others = card_sums[:, 52:53] - card_sums
        lane = lax.broadcasted_iota(jnp.int32, others.shape, 1)
        head = others.astype(bf16).astype(f32)
        middle = (others - head).astype(bf16).astype(f32)
        tail = others - head - middle
        split = jnp.where(lane < 64, head, jnp.where(lane < 128, middle, tail)).astype(bf16)
        folds[rows, :] = jnp.dot(split, card_marks, preferred_element_type=f32) + lhs[
            rows, :
        ].astype(f32)

    fold_sums(slice(0, LOCAL * BOARD_ROWS))
    level_rows = jnp.concatenate(
        [
            turned[pl.ds(128 * BOARD_BLOCKS * b + LEVEL_SLOT, OWNED, stride=SLOTS), :]
            for b in range(LOCAL)
        ]
        + [
            jnp.zeros((128 - LOCAL * OWNED, 128), f32),
        ],
        0,
    )
    level_columns = level_rows.T
    for q in range(LOCAL * OWNED):
        column = level_columns[:, q : q + 1]
        columns[q] = jnp.broadcast_to(column, (DEVICES, 128)).astype(bf16)

    card_load.wait()

    first_board = device_index() * LOCAL
    turn = first_board // RIVERS
    board_cards = [turn_cards[c, turn] for c in range(4)]
    low = cards[0:1, :]
    high = cards[1:2, :]
    free = low < 52
    for card in board_cards:
        free = free & (low != card) & (high != card)
    alive_turn = jnp.where(free, 1.0, 0.0).astype(f32)
    stake = stake_column(8)
    last_stake = PRE_POT + LINE_PUT[8]
    alive = []
    level_tiles = []
    for b in range(LOCAL):
        river = river_from(board_cards, first_board + b - turn * RIVERS)
        alive.append(jnp.where(free & (low != river) & (high != river), 1.0, 0.0).astype(f32))
        level_tiles.append(
            [
                jnp.concatenate(
                    [jnp.broadcast_to(level_rows[OWNED * b + k : OWNED * b + k + 1], (16, 128))] * 8,
                    0,
                ).astype(bf16)
                for k in range(OWNED)
            ]
        )
    marks[...] = jnp.zeros((128, 128), f32)
    for b in range(LOCAL):
        base = BOARD_ROWS * b
        for n in range(CHUNKS):
            tiles = range(2 * n, min(2 * n + 2, OWNED))
            lanes = slice(CHUNK * n, CHUNK * n + 128 * len(tiles))
            signs = []
            for k in range(OWNED):
                column = columns[OWNED * b + k]
                pieces = []
                for tile in tiles:
                    pair = pairs[128 * k : 128 * k + 128, 128 * tile : 128 * tile + 128]
                    pieces.append(jnp.clip(level_tiles[b][tile] - column, -1.0, 1.0) * pair)
                signs.append(jnp.concatenate(pieces, 1))
            ends[base : base + BOARD_ROWS, lanes] = jnp.dot(
                lhs[base : base + BOARD_ROWS, :],
                jnp.concatenate(signs, 0),
                preferred_element_type=f32,
            )

        def main_rows(sums):
            return {r: sums[base + 8 * i : base + 8 * i + 8, :] for i, r in enumerate(SENT)}

        def last_rows(sums):
            return {r: sums[base + 72 + i : base + 73 + i, :] for i, r in enumerate(SENT)}

        values = street_values(stake, main_rows(ends), main_rows(folds)) * alive[b]
        last = street_values(last_stake, last_rows(ends), last_rows(folds)) * alive[b]
        river_out[b, 0:8, :] = values
        river_out[b, 8:9, :] = last
        total = values if b == 0 else total + values
        last_total = last if b == 0 else last_total + last
    fold_total = (folds[82:83, :] + folds[83:84, :]) * alive_turn
    for k in range(OWNED):
        lanes = slice(128 * k, 128 * k + 128)
        marks[pl.ds(k, 8, stride=OWNED), :] = total[:, lanes]
        marks[88 + k : 89 + k, :] = last_total[:, lanes]
        marks[99 + k : 100 + k, :] = fold_total[:, lanes]
    sums_out[...] = marks[...].T


def boards(turn_cards, cards, recv, pairs):
    vmem = pl.BlockSpec(memory_space=pltpu.VMEM)
    hbm = pl.BlockSpec(memory_space=pl.ANY)
    recv, cards, pairs = keep(pltpu.VMEM, recv, cards, pairs)
    (turn_cards,) = keep(pltpu.HBM, turn_cards)
    return pl.pallas_call(
        board_kernel,
        in_specs=[hbm, vmem, vmem, vmem],
        out_specs=(vmem, vmem),
        out_shape=(
            jax.ShapeDtypeStruct((LOCAL, LINES, HANDS), jnp.float32),
            pltpu.VMEM((DEVICES, 128), jnp.float32),
        ),
        scratch_shapes=[
            pltpu.SMEM(turn_cards.shape, jnp.int32),
            pltpu.VMEM((DEVICES, PITCH, 128), jnp.float32),
            pltpu.VMEM((DEVICES * BLOCKS, 128), jnp.float32),
            pltpu.VMEM((LOCAL * BOARD_ROWS, HANDS), jnp.bfloat16),
            pltpu.VMEM((LOCAL * OWNED, DEVICES, 128), jnp.bfloat16),
            pltpu.VMEM((LOCAL * BOARD_ROWS, HANDS), jnp.float32),
            pltpu.VMEM((LOCAL * BOARD_ROWS, HANDS), jnp.float32),
            pltpu.VMEM((128, 128), jnp.float32),
            pltpu.SemaphoreType.DMA((1,)),
        ],
        compiler_params=pltpu.CompilerParams(vmem_limit_bytes=VMEM),
        name="board_values",
    )(turn_cards, cards, recv, pairs)


def turn_kernel(recv, out):
    group = DEVICES // TURNS
    line_sum = recv[pl.ds(0, TURNS, stride=group), :]
    for g in range(1, group):
        line_sum = line_sum + recv[pl.ds(g, TURNS, stride=group), :]
    line_sum = line_sum / float(RIVERS)
    leaf_values = {}
    for line, leaf in enumerate(ENDS):
        leaf_values[leaf] = pltpu.roll(line_sum, (128 - OWNED * line) % 128, 1)
    for f, leaf in enumerate(FOLDS):
        folder = TREE[leaf]["folder"]
        lost = PRE_POT + TREE[leaf]["put"][folder]
        fold = pltpu.roll(recv[pl.ds(f, TURNS, stride=group), :], 128 - OWNED * LINES, 1)
        leaf_values[leaf] = fold * (lost if folder == 1 else -lost)
    out[...] = back_up(leaf_values)[:, 0:OWNED]


def turns(recv):
    vmem = pl.BlockSpec(memory_space=pltpu.VMEM)
    (recv,) = keep(pltpu.VMEM, recv)
    return pl.pallas_call(
        turn_kernel,
        in_specs=[vmem],
        out_specs=vmem,
        out_shape=jax.ShapeDtypeStruct((TURNS, OWNED), jnp.float32),
        name="turn_values",
    )(recv)


def body(cum_turn, cum_river, opp_init, turn_cards, strength):
    low, high = hand_cards(HANDS)
    order = np.arange(HANDS).reshape(DEVICES, OWNED).T.reshape(-1)
    low, high = low[order], high[order]
    cards = np.zeros((8, HANDS), np.int32)
    cards[0], cards[1] = low, high
    deck = np.arange(128)
    marks = ((low[:, None] == deck) | (high[:, None] == deck)).astype(np.float32)
    pairs = np.zeros((HANDS + 256, HANDS), np.float32)
    pairs[0:HANDS] = marks @ marks.T == 0
    for copy in range(3):
        first = HANDS + 64 * copy
        pairs[first : first + 52] = marks.T[0:52]
        pairs[first + 52] = 0.5

    turn_cards = turn_cards.T
    packed = send(
        turn_cards, jnp.transpose(cum_turn, (0, 2, 1)), opp_init.T, strength, cum_river
    )
    packed = packed.reshape(DEVICES, BLOCKS, 128)
    recv = lax.all_to_all(packed, AXES, split_axis=0, concat_axis=0, tiled=True)
    river, sums = boards(
        turn_cards,
        jnp.asarray(cards),
        recv.reshape(DEVICES * BLOCKS, 128),
        jnp.asarray(pairs, jnp.bfloat16),
    )
    back = lax.all_to_all(
        sums.reshape(DEVICES, 1, 128), AXES, split_axis=0, concat_axis=0, tiled=True
    )
    river = river.reshape(LOCAL, LINES, OWNED, DEVICES)
    river_value = jnp.transpose(river, (0, 1, 3, 2)).reshape(LOCAL, LINES, HANDS)
    return river_value, turns(back.reshape(DEVICES, 128)).T


def solution(mesh):
    placed = (
        P(AXES, None, None),
        P(AXES, None, None, None),
        P(AXES, None),
        P(),
        P(AXES, None),
    )
    return jax.shard_map(
        body,
        mesh=mesh,
        in_specs=placed,
        out_specs=(P(AXES, None, None), P(AXES, None)),
        check_vma=False,
    )
```

```python
import jax
import jax.numpy as jnp
import numpy as np
from jax import lax
from jax.experimental import pallas as pl
from jax.experimental.pallas import tpu as pltpu
from jax.sharding import PartitionSpec as P

LIVE = 1326
RIVERS = 48
BETS = 4
PRE_POT = 2.0
UNROLL = True
GROUP = 3
AXES = ("board", "hand")

HANDS = 1408
DEVICES = 128
OWNED = HANDS // DEVICES
LINES = 9
ROWS = 13
BOARDS = 384
TURNS = 8
LOCAL = BOARDS // DEVICES
SLOTS = 80
BOARD_SLOTS = OWNED * SLOTS
BOARD_BLOCKS = 7
BLOCKS = LOCAL * BOARD_BLOCKS + 1
EXTRA = LOCAL * BOARD_BLOCKS
CHUNK = 256
CHUNKS = -(-HANDS // CHUNK)
PITCH = BLOCKS
BOARD_ROWS = 96
VMEM = 32 * 1024 * 1024


def grow_street(bet_cap):
    tree_nodes = []

    def add_leaf(leaf_kind, folder, put_zero, put_one):
        tree_nodes.append(
            {
                "kind": leaf_kind,
                "player": -1,
                "folder": folder,
                "put": (put_zero, put_one),
                "children": [],
            }
        )
        return len(tree_nodes) - 1

    def grow_node(player, bet_count, put_zero, put_one):
        position = len(tree_nodes)
        tree_nodes.append(
            {
                "kind": "act",
                "player": player,
                "folder": -1,
                "put": (put_zero, put_one),
                "children": [],
            }
        )
        own_put = put_zero if player == 0 else put_one
        rival_put = put_one if player == 0 else put_zero
        raised = rival_put + 1
        after_zero = raised if player == 0 else put_zero
        after_one = raised if player == 1 else put_one
        children = []
        if rival_put > own_put:
            children.append(add_leaf("fold", player, put_zero, put_one))
            children.append(add_leaf("end", -1, rival_put, rival_put))
        elif player == 0:
            children.append(grow_node(1, bet_count, put_zero, put_one))
        else:
            children.append(add_leaf("end", -1, put_zero, put_one))
        if bet_count < bet_cap:
            children.append(grow_node(1 - player, bet_count + 1, after_zero, after_one))
        tree_nodes[position]["children"] = children
        return position

    grow_node(0, 0, 0, 0)
    return tree_nodes


TREE = grow_street(BETS)
ENDS = [i for i, node in enumerate(TREE) if node["kind"] == "end"]
FOLDS = [i for i, node in enumerate(TREE) if node["kind"] == "fold"]
ROW_OF = {}
for _i, _node in enumerate(TREE):
    if _node["kind"] == "act" and _node["player"] == 1:
        for _child in _node["children"]:
            ROW_OF[_child] = len(ROW_OF)
REACH_ROW = dict(ROW_OF)
for _i, _node in enumerate(TREE):
    if _node["kind"] == "act" and _node["player"] == 0 and _i > 0:
        for _child in _node["children"]:
            REACH_ROW[_child] = REACH_ROW[_i]
LINE_PUT = [TREE[i]["put"][0] for i in ENDS]

SENT = [10, 11, 2, 3, 8, 5, 6, 7, 12]
SUM_OF = {4: ([5, 6], []), 9: ([10, 11, 12], []), 1: ([2, 3, 4], []), 0: ([7, 8, 9], [1])}


def hand_cards(hand_count):
    card_low = []
    card_high = []
    for low_card in range(52):
        for high_card in range(low_card + 1, 52):
            card_low.append(low_card)
            card_high.append(high_card)
    card_low = (card_low + [52] * hand_count)[:hand_count]
    card_high = (card_high + [53] * hand_count)[:hand_count]
    return np.array(card_low, np.int32), np.array(card_high, np.int32)


def back_up(leaf_values):
    values = dict(leaf_values)
    for node_id in reversed(range(len(TREE))):
        if TREE[node_id]["kind"] != "act":
            continue
        child_values = [values[child_id] for child_id in TREE[node_id]["children"]]
        merged = child_values[0]
        for other_value in child_values[1:]:
            if TREE[node_id]["player"] == 0:
                merged = jnp.maximum(merged, other_value)
            else:
                merged = merged + other_value
        values[node_id] = merged
    return values[0]


def node_rows():
    nodes = []
    for i, node in enumerate(TREE):
        if node["kind"] == "act" and node["player"] == 1:
            parent = REACH_ROW.get(i, -1)
            nodes.append((parent, [ROW_OF[c] for c in node["children"]]))
    return nodes


def sort_four(cards):
    a, b, c, d = cards
    a, b = jnp.minimum(a, b), jnp.maximum(a, b)
    c, d = jnp.minimum(c, d), jnp.maximum(c, d)
    a, c = jnp.minimum(a, c), jnp.maximum(a, c)
    b, d = jnp.minimum(b, d), jnp.maximum(b, d)
    b, c = jnp.minimum(b, c), jnp.maximum(b, c)
    return a, b, c, d


def river_from(cards, rank):
    river = rank
    for card in sort_four(cards):
        river = river + jnp.where(river >= card, 1, 0)
    return river


def device_index():
    return lax.axis_index("board") * lax.axis_size("hand") + lax.axis_index("hand")


def send_kernel(
    turn_cards_hbm,
    cum_turn_hbm,
    opp_init_hbm,
    strength_hbm,
    cum_river,
    pairs_hbm,
    out,
    pairs,
    turn_cards,
    cum_turn,
    opp_init,
    strength,
    cum,
    turn_rows,
    root,
    reach,
    rest,
    by_board,
    wide,
    sems,
):
    loads = [
        pltpu.make_async_copy(source, target, sems.at[i])
        for i, (source, target) in enumerate(
            [
                (cum_turn_hbm, cum_turn),
                (opp_init_hbm, opp_init),
                (turn_cards_hbm, turn_cards),
                (strength_hbm, strength),
            ]
        )
    ]
    fetches = []
    for i, first in enumerate(range(0, OWNED, GROUP)):
        part = pl.ds(first, min(GROUP, OWNED - first))
        fetches.append(
            pltpu.make_async_copy(cum_river.at[part], cum.at[part], sems.at[len(loads) + i])
        )
    pairs_load = pltpu.make_async_copy(pairs_hbm, pairs, sems.at[len(loads) + len(fetches)])
    for copy in loads + fetches + [pairs_load]:
        copy.start()
    f32 = jnp.float32
    first_hand = device_index() * OWNED
    hand = first_hand + lax.broadcasted_iota(jnp.int32, (16, 1), 0)
    low = jnp.zeros((16, 1), jnp.int32)
    for card in range(1, 52):
        low = low + jnp.where(hand >= card * (103 - card) // 2, 1, 0)
    high = hand - ((low * (103 - low)) >> 1) + low + 1
    board = lax.broadcasted_iota(jnp.int32, (1, BOARDS), 1)
    turn = jnp.zeros((1, BOARDS), jnp.int32)
    for q in range(1, TURNS):
        turn = turn + jnp.where(board >= RIVERS * q, 1, 0)
    loads[2].wait()
    cards = []
    for c in range(4):
        card = jnp.zeros((1, BOARDS), jnp.int32)
        for t in range(TURNS):
            card = jnp.where(turn == t, turn_cards[c, t], card)
        cards.append(card)
    river = river_from(cards, board - RIVERS * turn)
    free = hand < LIVE
    for card in cards:
        free = free & (low != card) & (high != card)
    alive_turn = jnp.where(free, 1.0, 0.0).astype(f32)
    alive = jnp.where(free & (low != river) & (high != river), 1.0, 0.0).astype(f32)

    turn_rows[...] = jnp.zeros(turn_rows.shape, f32)
    loads[0].wait()
    loads[1].wait()
    turn_rows[0 : OWNED * TURNS, 0:ROWS] = cum_turn[...].reshape(OWNED * TURNS, ROWS)
    turn_rows[128 : 128 + TURNS, 0:OWNED] = opp_init[...]
    by_row = turn_rows[0:128, :].T
    start = turn_rows[128:256, :].T[0:16]
    reach_map = {-1: None}
    lane = lax.broadcasted_iota(jnp.int32, (16, 128), 1)
    own = (lane >> 3) == lax.broadcasted_iota(jnp.int32, (16, 128), 0)
    stacked = [start]
    for parent, rows in node_rows():
        picked = [by_row[row : row + 1] for row in rows]
        summed = picked[0]
        for other in picked[1:]:
            summed = summed + other
        for row, value in zip(rows, picked):
            share = value / summed
            reach_map[row] = share if parent < 0 else reach_map[parent] * share
    for row in range(ROWS):
        stacked.append(jnp.where(own, reach_map[row], 0.0))
    lane_turn = lax.broadcasted_iota(jnp.int32, (128, BOARDS), 0)
    spread = jnp.where((lane_turn & 7) == turn, 1.0, 0.0).astype(f32)
    spread = jnp.where(lane_turn < OWNED * TURNS, spread, 0.0)
    spread_all = lax.dot_general(
        jnp.concatenate(stacked, 0),
        spread,
        (((1,), (0,)), ((), ())),
        precision=lax.Precision.HIGHEST,
        preferred_element_type=f32,
    )
    opponent = spread_all[0:16]
    alive_turn = alive_turn * opponent
    alive = alive * opponent
    spread_rows = spread_all[16:]
    for line, leaf in enumerate(ENDS):
        row = REACH_ROW[leaf]
        root[line] = spread_rows[16 * row : 16 * row + 16] * alive
    owner = (board * 171) >> 9
    fold_pick = owner & 7
    folded = jnp.zeros((16, BOARDS), f32)
    for f, leaf in enumerate(FOLDS):
        row = REACH_ROW[leaf]
        folded = jnp.where(fold_pick == f, spread_rows[16 * row : 16 * row + 16], folded)
    folded = folded * alive_turn
    fold_head = folded.astype(jnp.bfloat16).astype(f32)
    fold_tail = folded - fold_head
    loads[3].wait()
    level = strength[...].astype(f32)
    rest[...] = jnp.zeros((128, BOARDS), f32)
    rest[0:OWNED, :] = level
    rest[OWNED : 2 * OWNED, :] = fold_head[0:OWNED]
    rest[2 * OWNED : 3 * OWNED, :] = fold_tail[0:OWNED]
    reach[BOARD_SLOTS:, :] = jnp.zeros((128 * BOARD_BLOCKS - BOARD_SLOTS, BOARDS), f32)

    row_head = lax.broadcasted_iota(jnp.int32, (8, 1), 0)
    row_tail = lax.broadcasted_iota(jnp.int32, (8, 1), 0) + 8
    nodes = node_rows()

    def spread_over(row_ids, parts):
        merged = parts[-1]
        for (_, rows), part in reversed(list(zip(nodes[:-1], parts[:-1]))):
            merged = jnp.where(row_ids <= rows[-1], part, merged)
        return merged

    def one_hand(k):
        for line in range(LINES):
            x_head = cum[k, line, 0:8, :]
            x_tail = jnp.concatenate([cum[k, line, 8:13, :], jnp.ones((3, BOARDS), f32)], 0)
            rows = [cum[k, line, r : r + 1, :] for r in range(ROWS)]
            sums = []
            for _, ids in nodes:
                summed = rows[ids[0]]
                for r in ids[1:]:
                    summed = summed + rows[r]
                sums.append(summed)
            start = root[line, pl.ds(k, 1), :]
            q_head = x_head / spread_over(row_head, sums)
            q_tail = x_tail / spread_over(row_tail, sums)
            at_bet = start * q_head[1:2]
            at_raise = at_bet * q_head[4:5]
            at_reraise = start * q_tail[1:2]
            parents = [start, at_bet, at_raise, start, at_reraise]
            head = q_head * spread_over(row_head, parents)
            tail = q_tail * spread_over(row_tail, parents)
            mixed = jnp.where(
                row_head < 2,
                pltpu.roll(tail, 6, 0),
                jnp.where(row_head == 4, pltpu.roll(tail, 4, 0), head),
            )
            base = SLOTS * k
            reach[base + 8 * line : base + 8 * line + 8, :] = mixed
            last = base + 72 + line if line < 8 else BOARD_SLOTS + k
            reach[last : last + 1, :] = tail[4:5]

    for k in range(OWNED):
        if k % GROUP == 0:
            fetches[k // GROUP].wait()
        one_hand(k)

    for j in range(BOARD_BLOCKS):
        for i in range(LOCAL):
            by_board[j, 128 * i : 128 * i + 128, :] = reach[
                128 * j : 128 * j + 128, 128 * i : 128 * i + 128
            ].T
        for b in range(LOCAL):
            wide[pl.ds(BOARD_BLOCKS * b + j, DEVICES, stride=PITCH), :] = by_board[
                j, pl.ds(b, DEVICES, stride=LOCAL), :
            ]
    for i in range(LOCAL):
        by_board[BOARD_BLOCKS, 128 * i : 128 * i + 128, :] = rest[:, 128 * i : 128 * i + 128].T
    block = by_board[BOARD_BLOCKS, pl.ds(0, DEVICES, stride=LOCAL), :]
    for b in range(1, LOCAL):
        block = block + pltpu.roll(
            by_board[BOARD_BLOCKS, pl.ds(b, DEVICES, stride=LOCAL), :], 3 * OWNED * b, 1
        )
    wide[pl.ds(EXTRA, DEVICES, stride=PITCH), :] = block
    out[...] = wide[...].astype(jnp.bfloat16)
    pairs_load.wait()


def keep(space, *arrays):
    return [pltpu.with_memory_space_constraint(array, space) for array in arrays]


def send(turn_cards, cum_turn, opp_init, strength, cum_river, pairs):
    args = keep(pltpu.HBM, turn_cards, cum_turn, opp_init, strength, cum_river, pairs)
    vmem = pl.BlockSpec(memory_space=pltpu.VMEM)
    return pl.pallas_call(
        send_kernel,
        in_specs=[pl.BlockSpec(memory_space=pl.ANY)] * len(args),
        out_specs=(vmem, vmem),
        out_shape=(
            pltpu.VMEM((DEVICES * BLOCKS, 128), jnp.bfloat16),
            pltpu.VMEM(pairs.shape, jnp.bfloat16),
        ),
        scratch_shapes=[
            pltpu.SMEM(turn_cards.shape, jnp.int32),
            pltpu.VMEM(cum_turn.shape, jnp.float32),
            pltpu.VMEM(opp_init.shape, jnp.float32),
            pltpu.VMEM(strength.shape, jnp.int32),
            pltpu.VMEM((OWNED, LINES, ROWS, BOARDS), jnp.float32),
            pltpu.VMEM((256, 128), jnp.float32),
            pltpu.VMEM((LINES, 16, BOARDS), jnp.float32),
            pltpu.VMEM((128 * BOARD_BLOCKS, BOARDS), jnp.float32),
            pltpu.VMEM((128, BOARDS), jnp.float32),
            pltpu.VMEM((BOARD_BLOCKS + 1, BOARDS, 128), jnp.float32),
            pltpu.VMEM((DEVICES * PITCH, 128), jnp.float32),
            pltpu.SemaphoreType.DMA((5 + -(-OWNED // GROUP),)),
        ],
        compiler_params=pltpu.CompilerParams(vmem_limit_bytes=VMEM),
        name="send_reach",
    )(*args)


def stake_column(rows):
    line = lax.broadcasted_iota(jnp.int32, (rows, 1), 0)
    stake = jnp.zeros((rows, 1), jnp.float32)
    for i in range(rows):
        stake = jnp.where(line == i, PRE_POT + LINE_PUT[i], stake)
    return stake


def all_rows(sums):
    sums = dict(sums)
    for row, (plus, minus) in SUM_OF.items():
        total = sums[plus[0]]
        for other in plus[1:]:
            total = total + sums[other]
        for other in minus:
            total = total - sums[other]
        sums[row] = total
    return sums


def street_values(stake, end_sums, fold_sums):
    end_sums = all_rows(end_sums)
    fold_sums = all_rows(fold_sums)
    leaf_values = {}
    for leaf in ENDS:
        leaf_values[leaf] = end_sums[REACH_ROW[leaf]] * (stake + TREE[leaf]["put"][0])
    for leaf in FOLDS:
        folder = TREE[leaf]["folder"]
        lost = stake + TREE[leaf]["put"][folder]
        leaf_values[leaf] = fold_sums[REACH_ROW[leaf]] * (lost if folder == 1 else -lost)
    return back_up(leaf_values)


def board_kernel(
    turn_cards_hbm,
    cards,
    recv,
    pairs,
    river_out,
    sums_out,
    turn_cards,
    wide,
    turned,
    lhs,
    columns,
    ends,
    folds,
    marks,
    sems,
):
    f32 = jnp.float32
    bf16 = jnp.bfloat16
    card_load = pltpu.make_async_copy(turn_cards_hbm, turn_cards, sems.at[0])
    card_load.start()
    wide[...] = recv[...].astype(f32)
    for m in range(BLOCKS):
        block = wide[pl.ds(m, DEVICES, stride=PITCH), :]
        turned[128 * m : 128 * m + 128, :] = block.T
    for b in range(LOCAL):
        for k in range(OWNED):
            base = 128 * BOARD_BLOCKS * b + SLOTS * k
            parts = [turned[pl.ds(base + g, 8, stride=8), :] for g in range(8)]
            parts.append(turned[base + 72 : base + 80, :])
            parts.append(turned[base + 64 : base + 72, :])
            last = 128 * BOARD_BLOCKS * b + BOARD_SLOTS + k
            parts.append(turned[last : last + 1, :])
            for i in (1, 2):
                extra = 128 * EXTRA + OWNED * i + k
                parts.append(turned[extra : extra + 1, :])
            parts.append(jnp.zeros((13, 128), f32))
            lhs[BOARD_ROWS * b : BOARD_ROWS * (b + 1), 128 * k : 128 * k + 128] = jnp.concatenate(
                parts, 0
            ).astype(bf16)

    def fold_sums(rows):
        card_marks = pairs[HANDS : HANDS + 256, :]
        card_sums = lax.dot_general(
            lhs[rows, :], card_marks, (((1,), (1,)), ((), ())), preferred_element_type=f32
        )
        others = card_sums[:, 52:53] - card_sums
        lane = lax.broadcasted_iota(jnp.int32, others.shape, 1)
        head = others.astype(bf16).astype(f32)
        middle = (others - head).astype(bf16).astype(f32)
        tail = others - head - middle
        split = jnp.where(lane < 64, head, jnp.where(lane < 128, middle, tail)).astype(bf16)
        folds[rows, :] = jnp.dot(split, card_marks, preferred_element_type=f32) + lhs[
            rows, :
        ].astype(f32)

    fold_sums(slice(0, LOCAL * BOARD_ROWS))
    def level_row(b, k):
        first = 128 * EXTRA + 3 * OWNED * b + k
        return turned[first : first + 1, :]

    level_columns = wide[pl.ds(EXTRA, DEVICES, stride=PITCH), :]
    for q in range(LOCAL * OWNED):
        lane = 3 * OWNED * (q // OWNED) + q % OWNED
        column = level_columns[:, lane : lane + 1]
        columns[q] = jnp.broadcast_to(column, (DEVICES, 128)).astype(bf16)

    card_load.wait()

    first_board = device_index() * LOCAL
    turn = first_board // RIVERS
    board_cards = [turn_cards[c, turn] for c in range(4)]
    low = cards[0:1, :]
    high = cards[1:2, :]
    free = low < 52
    for card in board_cards:
        free = free & (low != card) & (high != card)
    alive_turn = jnp.where(free, 1.0, 0.0).astype(f32)
    stake = stake_column(8)
    last_stake = PRE_POT + LINE_PUT[8]
    alive = []
    level_tiles = []
    for b in range(LOCAL):
        river = river_from(board_cards, first_board + b - turn * RIVERS)
        alive.append(jnp.where(free & (low != river) & (high != river), 1.0, 0.0).astype(f32))
        level_tiles.append(
            [
                jnp.concatenate(
                    [jnp.broadcast_to(level_row(b, k), (16, 128))] * 8,
                    0,
                ).astype(bf16)
                for k in range(OWNED)
            ]
        )
    marks[...] = jnp.zeros((128, 128), f32)
    for b in range(LOCAL):
        base = BOARD_ROWS * b
        for n in range(CHUNKS):
            tiles = range(2 * n, min(2 * n + 2, OWNED))
            lanes = slice(CHUNK * n, CHUNK * n + 128 * len(tiles))
            signs = []
            for k in range(OWNED):
                column = columns[OWNED * b + k]
                pieces = []
                for tile in tiles:
                    pair = pairs[128 * k : 128 * k + 128, 128 * tile : 128 * tile + 128]
                    pieces.append(jnp.clip(level_tiles[b][tile] - column, -1.0, 1.0) * pair)
                signs.append(jnp.concatenate(pieces, 1))
            ends[base : base + BOARD_ROWS, lanes] = jnp.dot(
                lhs[base : base + BOARD_ROWS, :],
                jnp.concatenate(signs, 0),
                preferred_element_type=f32,
            )

        def main_rows(sums):
            return {r: sums[base + 8 * i : base + 8 * i + 8, :] for i, r in enumerate(SENT)}

        def last_rows(sums):
            return {r: sums[base + 72 + i : base + 73 + i, :] for i, r in enumerate(SENT)}

        values = street_values(stake, main_rows(ends), main_rows(folds)) * alive[b]
        last = street_values(last_stake, last_rows(ends), last_rows(folds)) * alive[b]
        river_out[b, 0:8, :] = values
        river_out[b, 8:9, :] = last
        total = values if b == 0 else total + values
        last_total = last if b == 0 else last_total + last
    fold_total = (folds[81:82, :] + folds[82:83, :]) * alive_turn
    for k in range(OWNED):
        lanes = slice(128 * k, 128 * k + 128)
        marks[pl.ds(k, 8, stride=OWNED), :] = total[:, lanes]
        marks[88 + k : 89 + k, :] = last_total[:, lanes]
        marks[99 + k : 100 + k, :] = fold_total[:, lanes]
    sums_out[...] = marks[...].T


def boards(turn_cards, cards, recv, pairs):
    vmem = pl.BlockSpec(memory_space=pltpu.VMEM)
    hbm = pl.BlockSpec(memory_space=pl.ANY)
    recv, cards, pairs = keep(pltpu.VMEM, recv, cards, pairs)
    (turn_cards,) = keep(pltpu.HBM, turn_cards)
    return pl.pallas_call(
        board_kernel,
        in_specs=[hbm, vmem, vmem, vmem],
        out_specs=(vmem, vmem),
        out_shape=(
            jax.ShapeDtypeStruct((LOCAL, LINES, HANDS), jnp.float32),
            pltpu.VMEM((DEVICES, 128), jnp.float32),
        ),
        scratch_shapes=[
            pltpu.SMEM(turn_cards.shape, jnp.int32),
            pltpu.VMEM((DEVICES * PITCH, 128), jnp.float32),
            pltpu.VMEM((DEVICES * BLOCKS, 128), jnp.float32),
            pltpu.VMEM((LOCAL * BOARD_ROWS, HANDS), jnp.bfloat16),
            pltpu.VMEM((LOCAL * OWNED, DEVICES, 128), jnp.bfloat16),
            pltpu.VMEM((LOCAL * BOARD_ROWS, HANDS), jnp.float32),
            pltpu.VMEM((LOCAL * BOARD_ROWS, HANDS), jnp.float32),
            pltpu.VMEM((128, 128), jnp.float32),
            pltpu.SemaphoreType.DMA((1,)),
        ],
        compiler_params=pltpu.CompilerParams(vmem_limit_bytes=VMEM),
        name="board_values",
    )(turn_cards, cards, recv, pairs)


def turn_kernel(recv, out):
    group = DEVICES // TURNS
    line_sum = recv[pl.ds(0, TURNS, stride=group), :]
    for g in range(1, group):
        line_sum = line_sum + recv[pl.ds(g, TURNS, stride=group), :]
    line_sum = line_sum / float(RIVERS)
    leaf_values = {}
    for line, leaf in enumerate(ENDS):
        leaf_values[leaf] = pltpu.roll(line_sum, (128 - OWNED * line) % 128, 1)
    for f, leaf in enumerate(FOLDS):
        folder = TREE[leaf]["folder"]
        lost = PRE_POT + TREE[leaf]["put"][folder]
        fold = pltpu.roll(recv[pl.ds(f, TURNS, stride=group), :], 128 - OWNED * LINES, 1)
        leaf_values[leaf] = fold * (lost if folder == 1 else -lost)
    out[...] = back_up(leaf_values)[:, 0:OWNED]


def turns(recv):
    vmem = pl.BlockSpec(memory_space=pltpu.VMEM)
    (recv,) = keep(pltpu.VMEM, recv)
    return pl.pallas_call(
        turn_kernel,
        in_specs=[vmem],
        out_specs=vmem,
        out_shape=jax.ShapeDtypeStruct((TURNS, OWNED), jnp.float32),
        name="turn_values",
    )(recv)


def body(cum_turn, cum_river, opp_init, turn_cards, strength):
    low, high = hand_cards(HANDS)
    order = np.arange(HANDS).reshape(DEVICES, OWNED).T.reshape(-1)
    low, high = low[order], high[order]
    cards = np.zeros((8, HANDS), np.int32)
    cards[0], cards[1] = low, high
    deck = np.arange(128)
    marks = ((low[:, None] == deck) | (high[:, None] == deck)).astype(np.float32)
    pairs = np.zeros((HANDS + 256, HANDS), np.float32)
    pairs[0:HANDS] = marks @ marks.T == 0
    for copy in range(3):
        first = HANDS + 64 * copy
        pairs[first : first + 52] = marks.T[0:52]
        pairs[first + 52] = 0.5

    turn_cards = turn_cards.T
    packed, pairs = send(
        turn_cards,
        jnp.transpose(cum_turn, (0, 2, 1)),
        opp_init.T,
        strength,
        cum_river,
        jnp.asarray(pairs, jnp.bfloat16),
    )
    packed = packed.reshape(DEVICES, BLOCKS // 2, 2, 128)
    recv = lax.all_to_all(packed, AXES, split_axis=0, concat_axis=0, tiled=True)
    river, sums = boards(
        turn_cards,
        jnp.asarray(cards),
        recv.reshape(DEVICES * BLOCKS, 128),
        pairs,
    )
    back = lax.all_to_all(
        sums.reshape(DEVICES, 1, 128), AXES, split_axis=0, concat_axis=0, tiled=True
    )
    river = river.reshape(LOCAL, LINES, OWNED, DEVICES)
    river_value = jnp.transpose(river, (0, 1, 3, 2)).reshape(LOCAL, LINES, HANDS)
    return river_value, turns(back.reshape(DEVICES, 128)).T


def solution(mesh):
    placed = (
        P(AXES, None, None),
        P(AXES, None, None, None),
        P(AXES, None),
        P(),
        P(AXES, None),
    )
    return jax.shard_map(
        body,
        mesh=mesh,
        in_specs=placed,
        out_specs=(P(AXES, None, None), P(AXES, None)),
        check_vma=False,
    )
```

```python
import jax
import jax.numpy as jnp
import numpy as np
from jax import lax
from jax.experimental import pallas as pl
from jax.experimental.pallas import tpu as pltpu
from jax.sharding import PartitionSpec as P

LIVE = 1326
RIVERS = 48
BETS = 4
PRE_POT = 2.0
UNROLL = True
GROUP = 6
AXES = ("board", "hand")

HANDS = 1408
DEVICES = 128
OWNED = HANDS // DEVICES
LINES = 9
ROWS = 13
BOARDS = 384
TURNS = 8
LOCAL = BOARDS // DEVICES
SLOTS = 80
BOARD_SLOTS = OWNED * SLOTS
BOARD_BLOCKS = 7
BLOCKS = LOCAL * BOARD_BLOCKS + 1
EXTRA = LOCAL * BOARD_BLOCKS
CHUNK = 256
CHUNKS = -(-HANDS // CHUNK)
PITCH = BLOCKS
BOARD_ROWS = 96
VMEM = 32 * 1024 * 1024


def grow_street(bet_cap):
    tree_nodes = []

    def add_leaf(leaf_kind, folder, put_zero, put_one):
        tree_nodes.append(
            {
                "kind": leaf_kind,
                "player": -1,
                "folder": folder,
                "put": (put_zero, put_one),
                "children": [],
            }
        )
        return len(tree_nodes) - 1

    def grow_node(player, bet_count, put_zero, put_one):
        position = len(tree_nodes)
        tree_nodes.append(
            {
                "kind": "act",
                "player": player,
                "folder": -1,
                "put": (put_zero, put_one),
                "children": [],
            }
        )
        own_put = put_zero if player == 0 else put_one
        rival_put = put_one if player == 0 else put_zero
        raised = rival_put + 1
        after_zero = raised if player == 0 else put_zero
        after_one = raised if player == 1 else put_one
        children = []
        if rival_put > own_put:
            children.append(add_leaf("fold", player, put_zero, put_one))
            children.append(add_leaf("end", -1, rival_put, rival_put))
        elif player == 0:
            children.append(grow_node(1, bet_count, put_zero, put_one))
        else:
            children.append(add_leaf("end", -1, put_zero, put_one))
        if bet_count < bet_cap:
            children.append(grow_node(1 - player, bet_count + 1, after_zero, after_one))
        tree_nodes[position]["children"] = children
        return position

    grow_node(0, 0, 0, 0)
    return tree_nodes


TREE = grow_street(BETS)
ENDS = [i for i, node in enumerate(TREE) if node["kind"] == "end"]
FOLDS = [i for i, node in enumerate(TREE) if node["kind"] == "fold"]
ROW_OF = {}
for _i, _node in enumerate(TREE):
    if _node["kind"] == "act" and _node["player"] == 1:
        for _child in _node["children"]:
            ROW_OF[_child] = len(ROW_OF)
REACH_ROW = dict(ROW_OF)
for _i, _node in enumerate(TREE):
    if _node["kind"] == "act" and _node["player"] == 0 and _i > 0:
        for _child in _node["children"]:
            REACH_ROW[_child] = REACH_ROW[_i]
LINE_PUT = [TREE[i]["put"][0] for i in ENDS]

SENT = [10, 11, 2, 3, 8, 5, 6, 7, 12]
SUM_OF = {4: ([5, 6], []), 9: ([10, 11, 12], []), 1: ([2, 3, 4], []), 0: ([7, 8, 9], [1])}


def hand_cards(hand_count):
    card_low = []
    card_high = []
    for low_card in range(52):
        for high_card in range(low_card + 1, 52):
            card_low.append(low_card)
            card_high.append(high_card)
    card_low = (card_low + [52] * hand_count)[:hand_count]
    card_high = (card_high + [53] * hand_count)[:hand_count]
    return np.array(card_low, np.int32), np.array(card_high, np.int32)


def back_up(leaf_values):
    values = dict(leaf_values)
    for node_id in reversed(range(len(TREE))):
        if TREE[node_id]["kind"] != "act":
            continue
        child_values = [values[child_id] for child_id in TREE[node_id]["children"]]
        merged = child_values[0]
        for other_value in child_values[1:]:
            if TREE[node_id]["player"] == 0:
                merged = jnp.maximum(merged, other_value)
            else:
                merged = merged + other_value
        values[node_id] = merged
    return values[0]


def node_rows():
    nodes = []
    for i, node in enumerate(TREE):
        if node["kind"] == "act" and node["player"] == 1:
            parent = REACH_ROW.get(i, -1)
            nodes.append((parent, [ROW_OF[c] for c in node["children"]]))
    return nodes


def sort_four(cards):
    a, b, c, d = cards
    a, b = jnp.minimum(a, b), jnp.maximum(a, b)
    c, d = jnp.minimum(c, d), jnp.maximum(c, d)
    a, c = jnp.minimum(a, c), jnp.maximum(a, c)
    b, d = jnp.minimum(b, d), jnp.maximum(b, d)
    b, c = jnp.minimum(b, c), jnp.maximum(b, c)
    return a, b, c, d


def river_from(cards, rank):
    river = rank
    for card in sort_four(cards):
        river = river + jnp.where(river >= card, 1, 0)
    return river


def device_index():
    return lax.axis_index("board") * lax.axis_size("hand") + lax.axis_index("hand")


def send_kernel(
    turn_cards_hbm,
    cum_turn_hbm,
    opp_init_hbm,
    strength_hbm,
    cum_river,
    pairs_hbm,
    out,
    pairs,
    turn_cards,
    cum_turn,
    opp_init,
    strength,
    cum,
    turn_rows,
    root,
    reach,
    rest,
    by_board,
    wide,
    sems,
):
    loads = [
        pltpu.make_async_copy(source, target, sems.at[i])
        for i, (source, target) in enumerate(
            [
                (cum_turn_hbm, cum_turn),
                (opp_init_hbm, opp_init),
                (turn_cards_hbm, turn_cards),
                (strength_hbm, strength),
            ]
        )
    ]
    fetches = []
    for i, first in enumerate(range(0, OWNED, GROUP)):
        part = pl.ds(first, min(GROUP, OWNED - first))
        fetches.append(
            pltpu.make_async_copy(cum_river.at[part], cum.at[part], sems.at[len(loads) + i])
        )
    pairs_load = pltpu.make_async_copy(pairs_hbm, pairs, sems.at[len(loads) + len(fetches)])
    for copy in loads + fetches + [pairs_load]:
        copy.start()
    f32 = jnp.float32
    first_hand = device_index() * OWNED
    hand = first_hand + lax.broadcasted_iota(jnp.int32, (16, 1), 0)
    low = jnp.zeros((16, 1), jnp.int32)
    for card in range(1, 52):
        low = low + jnp.where(hand >= card * (103 - card) // 2, 1, 0)
    high = hand - ((low * (103 - low)) >> 1) + low + 1
    board = lax.broadcasted_iota(jnp.int32, (1, BOARDS), 1)
    turn = jnp.zeros((1, BOARDS), jnp.int32)
    for q in range(1, TURNS):
        turn = turn + jnp.where(board >= RIVERS * q, 1, 0)
    loads[2].wait()
    cards = []
    for c in range(4):
        card = jnp.zeros((1, BOARDS), jnp.int32)
        for t in range(TURNS):
            card = jnp.where(turn == t, turn_cards[c, t], card)
        cards.append(card)
    river = river_from(cards, board - RIVERS * turn)
    free = hand < LIVE
    for card in cards:
        free = free & (low != card) & (high != card)
    alive_turn = jnp.where(free, 1.0, 0.0).astype(f32)
    alive = jnp.where(free & (low != river) & (high != river), 1.0, 0.0).astype(f32)

    turn_rows[...] = jnp.zeros(turn_rows.shape, f32)
    loads[0].wait()
    loads[1].wait()
    turn_rows[0 : OWNED * TURNS, 0:ROWS] = cum_turn[...].reshape(OWNED * TURNS, ROWS)
    turn_rows[128 : 128 + TURNS, 0:OWNED] = opp_init[...]
    by_row = turn_rows[0:128, :].T
    start = turn_rows[128:256, :].T[0:16]
    reach_map = {-1: None}
    lane = lax.broadcasted_iota(jnp.int32, (16, 128), 1)
    own = (lane >> 3) == lax.broadcasted_iota(jnp.int32, (16, 128), 0)
    stacked = [start]
    for parent, rows in node_rows():
        picked = [by_row[row : row + 1] for row in rows]
        summed = picked[0]
        for other in picked[1:]:
            summed = summed + other
        for row, value in zip(rows, picked):
            share = value / summed
            reach_map[row] = share if parent < 0 else reach_map[parent] * share
    for row in range(ROWS):
        stacked.append(jnp.where(own, reach_map[row], 0.0))
    lane_turn = lax.broadcasted_iota(jnp.int32, (128, BOARDS), 0)
    spread = jnp.where((lane_turn & 7) == turn, 1.0, 0.0).astype(f32)
    spread = jnp.where(lane_turn < OWNED * TURNS, spread, 0.0)
    spread_all = lax.dot_general(
        jnp.concatenate(stacked, 0),
        spread,
        (((1,), (0,)), ((), ())),
        precision=lax.Precision.HIGHEST,
        preferred_element_type=f32,
    )
    opponent = spread_all[0:16]
    alive_turn = alive_turn * opponent
    alive = alive * opponent
    spread_rows = spread_all[16:]
    for line, leaf in enumerate(ENDS):
        row = REACH_ROW[leaf]
        root[line] = spread_rows[16 * row : 16 * row + 16] * alive
    owner = (board * 171) >> 9
    fold_pick = owner & 7
    folded = jnp.zeros((16, BOARDS), f32)
    for f, leaf in enumerate(FOLDS):
        row = REACH_ROW[leaf]
        folded = jnp.where(fold_pick == f, spread_rows[16 * row : 16 * row + 16], folded)
    folded = folded * alive_turn
    fold_head = folded.astype(jnp.bfloat16).astype(f32)
    fold_tail = folded - fold_head
    loads[3].wait()
    level = strength[...].astype(f32)
    rest[...] = jnp.zeros((128, BOARDS), f32)
    rest[0:OWNED, :] = level
    rest[OWNED : 2 * OWNED, :] = fold_head[0:OWNED]
    rest[2 * OWNED : 3 * OWNED, :] = fold_tail[0:OWNED]
    reach[BOARD_SLOTS:, :] = jnp.zeros((128 * BOARD_BLOCKS - BOARD_SLOTS, BOARDS), f32)

    row_head = lax.broadcasted_iota(jnp.int32, (8, 1), 0)
    row_tail = lax.broadcasted_iota(jnp.int32, (8, 1), 0) + 8
    nodes = node_rows()

    def spread_over(row_ids, parts):
        merged = parts[-1]
        for (_, rows), part in reversed(list(zip(nodes[:-1], parts[:-1]))):
            merged = jnp.where(row_ids <= rows[-1], part, merged)
        return merged

    def one_hand(k):
        for line in range(LINES):
            x_head = cum[k, line, 0:8, :]
            x_tail = jnp.concatenate([cum[k, line, 8:13, :], jnp.ones((3, BOARDS), f32)], 0)
            rows = [cum[k, line, r : r + 1, :] for r in range(ROWS)]
            sums = []
            for _, ids in nodes:
                summed = rows[ids[0]]
                for r in ids[1:]:
                    summed = summed + rows[r]
                sums.append(summed)
            start = root[line, pl.ds(k, 1), :]
            q_head = x_head / spread_over(row_head, sums)
            q_tail = x_tail / spread_over(row_tail, sums)
            at_bet = start * q_head[1:2]
            at_raise = at_bet * q_head[4:5]
            at_reraise = start * q_tail[1:2]
            parents = [start, at_bet, at_raise, start, at_reraise]
            head = q_head * spread_over(row_head, parents)
            tail = q_tail * spread_over(row_tail, parents)
            mixed = jnp.where(
                row_head < 2,
                pltpu.roll(tail, 6, 0),
                jnp.where(row_head == 4, pltpu.roll(tail, 4, 0), head),
            )
            base = SLOTS * k
            reach[base + 8 * line : base + 8 * line + 8, :] = mixed
            last = base + 72 + line if line < 8 else BOARD_SLOTS + k
            reach[last : last + 1, :] = tail[4:5]

    for k in range(OWNED):
        if k % GROUP == 0:
            fetches[k // GROUP].wait()
        one_hand(k)

    for j in range(BOARD_BLOCKS):
        for i in range(LOCAL):
            by_board[j, 128 * i : 128 * i + 128, :] = reach[
                128 * j : 128 * j + 128, 128 * i : 128 * i + 128
            ].T
        for b in range(LOCAL):
            wide[pl.ds(BOARD_BLOCKS * b + j, DEVICES, stride=PITCH), :] = by_board[
                j, pl.ds(b, DEVICES, stride=LOCAL), :
            ]
    for i in range(LOCAL):
        by_board[BOARD_BLOCKS, 128 * i : 128 * i + 128, :] = rest[:, 128 * i : 128 * i + 128].T
    block = by_board[BOARD_BLOCKS, pl.ds(0, DEVICES, stride=LOCAL), :]
    for b in range(1, LOCAL):
        block = block + pltpu.roll(
            by_board[BOARD_BLOCKS, pl.ds(b, DEVICES, stride=LOCAL), :], 3 * OWNED * b, 1
        )
    wide[pl.ds(EXTRA, DEVICES, stride=PITCH), :] = block
    out[...] = wide[...].astype(jnp.bfloat16)
    pairs_load.wait()


def keep(space, *arrays):
    return [pltpu.with_memory_space_constraint(array, space) for array in arrays]


def send(turn_cards, cum_turn, opp_init, strength, cum_river, pairs):
    args = keep(pltpu.HBM, turn_cards, cum_turn, opp_init, strength, cum_river, pairs)
    vmem = pl.BlockSpec(memory_space=pltpu.VMEM)
    return pl.pallas_call(
        send_kernel,
        in_specs=[pl.BlockSpec(memory_space=pl.ANY)] * len(args),
        out_specs=(vmem, vmem),
        out_shape=(
            pltpu.VMEM((DEVICES * BLOCKS, 128), jnp.bfloat16),
            pltpu.VMEM(pairs.shape, jnp.bfloat16),
        ),
        scratch_shapes=[
            pltpu.SMEM(turn_cards.shape, jnp.int32),
            pltpu.VMEM(cum_turn.shape, jnp.float32),
            pltpu.VMEM(opp_init.shape, jnp.float32),
            pltpu.VMEM(strength.shape, jnp.int32),
            pltpu.VMEM((OWNED, LINES, ROWS, BOARDS), jnp.float32),
            pltpu.VMEM((256, 128), jnp.float32),
            pltpu.VMEM((LINES, 16, BOARDS), jnp.float32),
            pltpu.VMEM((128 * BOARD_BLOCKS, BOARDS), jnp.float32),
            pltpu.VMEM((128, BOARDS), jnp.float32),
            pltpu.VMEM((BOARD_BLOCKS + 1, BOARDS, 128), jnp.float32),
            pltpu.VMEM((DEVICES * PITCH, 128), jnp.float32),
            pltpu.SemaphoreType.DMA((5 + -(-OWNED // GROUP),)),
        ],
        compiler_params=pltpu.CompilerParams(vmem_limit_bytes=VMEM),
        name="send_reach",
    )(*args)


def stake_column(rows):
    line = lax.broadcasted_iota(jnp.int32, (rows, 1), 0)
    stake = jnp.zeros((rows, 1), jnp.float32)
    for i in range(rows):
        stake = jnp.where(line == i, PRE_POT + LINE_PUT[i], stake)
    return stake


def all_rows(sums):
    sums = dict(sums)
    for row, (plus, minus) in SUM_OF.items():
        total = sums[plus[0]]
        for other in plus[1:]:
            total = total + sums[other]
        for other in minus:
            total = total - sums[other]
        sums[row] = total
    return sums


def street_values(stake, end_sums, fold_sums):
    end_sums = all_rows(end_sums)
    fold_sums = all_rows(fold_sums)
    leaf_values = {}
    for leaf in ENDS:
        leaf_values[leaf] = end_sums[REACH_ROW[leaf]] * (stake + TREE[leaf]["put"][0])
    for leaf in FOLDS:
        folder = TREE[leaf]["folder"]
        lost = stake + TREE[leaf]["put"][folder]
        leaf_values[leaf] = fold_sums[REACH_ROW[leaf]] * (lost if folder == 1 else -lost)
    return back_up(leaf_values)


def board_kernel(
    turn_cards_hbm,
    cards,
    recv,
    pairs,
    river_out,
    sums_out,
    turn_cards,
    wide,
    turned,
    lhs,
    columns,
    ends,
    folds,
    marks,
    sems,
):
    f32 = jnp.float32
    bf16 = jnp.bfloat16
    card_load = pltpu.make_async_copy(turn_cards_hbm, turn_cards, sems.at[0])
    card_load.start()
    wide[...] = recv[...].astype(f32)
    for m in range(BLOCKS):
        block = wide[pl.ds(m, DEVICES, stride=PITCH), :]
        turned[128 * m : 128 * m + 128, :] = block.T
    for b in range(LOCAL):
        for k in range(OWNED):
            base = 128 * BOARD_BLOCKS * b + SLOTS * k
            parts = [turned[pl.ds(base + g, 8, stride=8), :] for g in range(8)]
            parts.append(turned[base + 72 : base + 80, :])
            parts.append(turned[base + 64 : base + 72, :])
            last = 128 * BOARD_BLOCKS * b + BOARD_SLOTS + k
            parts.append(turned[last : last + 1, :])
            for i in (1, 2):
                extra = 128 * EXTRA + OWNED * i + k
                parts.append(turned[extra : extra + 1, :])
            parts.append(jnp.zeros((13, 128), f32))
            lhs[BOARD_ROWS * b : BOARD_ROWS * (b + 1), 128 * k : 128 * k + 128] = jnp.concatenate(
                parts, 0
            ).astype(bf16)

    def fold_sums(rows):
        card_marks = pairs[HANDS : HANDS + 256, :]
        card_sums = lax.dot_general(
            lhs[rows, :], card_marks, (((1,), (1,)), ((), ())), preferred_element_type=f32
        )
        others = card_sums[:, 52:53] - card_sums
        lane = lax.broadcasted_iota(jnp.int32, others.shape, 1)
        head = others.astype(bf16).astype(f32)
        middle = (others - head).astype(bf16).astype(f32)
        tail = others - head - middle
        split = jnp.where(lane < 64, head, jnp.where(lane < 128, middle, tail)).astype(bf16)
        folds[rows, :] = jnp.dot(split, card_marks, preferred_element_type=f32) + lhs[
            rows, :
        ].astype(f32)

    fold_sums(slice(0, LOCAL * BOARD_ROWS))
    def level_row(b, k):
        first = 128 * EXTRA + 3 * OWNED * b + k
        return turned[first : first + 1, :]

    level_columns = wide[pl.ds(EXTRA, DEVICES, stride=PITCH), :]
    for q in range(LOCAL * OWNED):
        lane = 3 * OWNED * (q // OWNED) + q % OWNED
        column = level_columns[:, lane : lane + 1]
        columns[q] = jnp.broadcast_to(column, (DEVICES, 128)).astype(bf16)

    card_load.wait()

    first_board = device_index() * LOCAL
    turn = first_board // RIVERS
    board_cards = [turn_cards[c, turn] for c in range(4)]
    low = cards[0:1, :]
    high = cards[1:2, :]
    free = low < 52
    for card in board_cards:
        free = free & (low != card) & (high != card)
    alive_turn = jnp.where(free, 1.0, 0.0).astype(f32)
    stake = stake_column(8)
    last_stake = PRE_POT + LINE_PUT[8]
    alive = []
    level_tiles = []
    for b in range(LOCAL):
        river = river_from(board_cards, first_board + b - turn * RIVERS)
        alive.append(jnp.where(free & (low != river) & (high != river), 1.0, 0.0).astype(f32))
        level_tiles.append(
            [
                jnp.concatenate(
                    [jnp.broadcast_to(level_row(b, k), (16, 128))] * 8,
                    0,
                ).astype(bf16)
                for k in range(OWNED)
            ]
        )
    marks[...] = jnp.zeros((128, 128), f32)
    for b in range(LOCAL):
        base = BOARD_ROWS * b
        for n in range(CHUNKS):
            tiles = range(2 * n, min(2 * n + 2, OWNED))
            lanes = slice(CHUNK * n, CHUNK * n + 128 * len(tiles))
            signs = []
            for k in range(OWNED):
                column = columns[OWNED * b + k]
                pieces = []
                for tile in tiles:
                    pair = pairs[128 * k : 128 * k + 128, 128 * tile : 128 * tile + 128]
                    pieces.append(jnp.clip(level_tiles[b][tile] - column, -1.0, 1.0) * pair)
                signs.append(jnp.concatenate(pieces, 1))
            ends[base : base + BOARD_ROWS, lanes] = jnp.dot(
                lhs[base : base + BOARD_ROWS, :],
                jnp.concatenate(signs, 0),
                preferred_element_type=f32,
            )

        def main_rows(sums):
            return {r: sums[base + 8 * i : base + 8 * i + 8, :] for i, r in enumerate(SENT)}

        def last_rows(sums):
            return {r: sums[base + 72 + i : base + 73 + i, :] for i, r in enumerate(SENT)}

        values = street_values(stake, main_rows(ends), main_rows(folds)) * alive[b]
        last = street_values(last_stake, last_rows(ends), last_rows(folds)) * alive[b]
        river_out[b, 0:8, :] = values
        river_out[b, 8:9, :] = last
        total = values if b == 0 else total + values
        last_total = last if b == 0 else last_total + last
    fold_total = (folds[81:82, :] + folds[82:83, :]) * alive_turn
    for k in range(OWNED):
        lanes = slice(128 * k, 128 * k + 128)
        marks[pl.ds(k, 8, stride=OWNED), :] = total[:, lanes]
        marks[88 + k : 89 + k, :] = last_total[:, lanes]
        marks[99 + k : 100 + k, :] = fold_total[:, lanes]
    sums_out[...] = marks[...].T


def boards(turn_cards, cards, recv, pairs):
    vmem = pl.BlockSpec(memory_space=pltpu.VMEM)
    hbm = pl.BlockSpec(memory_space=pl.ANY)
    recv, cards, pairs = keep(pltpu.VMEM, recv, cards, pairs)
    (turn_cards,) = keep(pltpu.HBM, turn_cards)
    return pl.pallas_call(
        board_kernel,
        in_specs=[hbm, vmem, vmem, vmem],
        out_specs=(vmem, vmem),
        out_shape=(
            jax.ShapeDtypeStruct((LOCAL, LINES, HANDS), jnp.float32),
            pltpu.VMEM((DEVICES, 128), jnp.float32),
        ),
        scratch_shapes=[
            pltpu.SMEM(turn_cards.shape, jnp.int32),
            pltpu.VMEM((DEVICES * PITCH, 128), jnp.float32),
            pltpu.VMEM((DEVICES * BLOCKS, 128), jnp.float32),
            pltpu.VMEM((LOCAL * BOARD_ROWS, HANDS), jnp.bfloat16),
            pltpu.VMEM((LOCAL * OWNED, DEVICES, 128), jnp.bfloat16),
            pltpu.VMEM((LOCAL * BOARD_ROWS, HANDS), jnp.float32),
            pltpu.VMEM((LOCAL * BOARD_ROWS, HANDS), jnp.float32),
            pltpu.VMEM((128, 128), jnp.float32),
            pltpu.SemaphoreType.DMA((1,)),
        ],
        compiler_params=pltpu.CompilerParams(vmem_limit_bytes=VMEM),
        name="board_values",
    )(turn_cards, cards, recv, pairs)


def turn_kernel(recv, out):
    group = DEVICES // TURNS
    line_sum = recv[pl.ds(0, TURNS, stride=group), :]
    for g in range(1, group):
        line_sum = line_sum + recv[pl.ds(g, TURNS, stride=group), :]
    line_sum = line_sum / float(RIVERS)
    leaf_values = {}
    for line, leaf in enumerate(ENDS):
        leaf_values[leaf] = pltpu.roll(line_sum, (128 - OWNED * line) % 128, 1)
    for f, leaf in enumerate(FOLDS):
        folder = TREE[leaf]["folder"]
        lost = PRE_POT + TREE[leaf]["put"][folder]
        fold = pltpu.roll(recv[pl.ds(f, TURNS, stride=group), :], 128 - OWNED * LINES, 1)
        leaf_values[leaf] = fold * (lost if folder == 1 else -lost)
    out[...] = back_up(leaf_values)[:, 0:OWNED]


def turns(recv):
    vmem = pl.BlockSpec(memory_space=pltpu.VMEM)
    (recv,) = keep(pltpu.VMEM, recv)
    return pl.pallas_call(
        turn_kernel,
        in_specs=[vmem],
        out_specs=vmem,
        out_shape=jax.ShapeDtypeStruct((TURNS, OWNED), jnp.float32),
        name="turn_values",
    )(recv)


def body(cum_turn, cum_river, opp_init, turn_cards, strength):
    low, high = hand_cards(HANDS)
    order = np.arange(HANDS).reshape(DEVICES, OWNED).T.reshape(-1)
    low, high = low[order], high[order]
    cards = np.zeros((8, HANDS), np.int32)
    cards[0], cards[1] = low, high
    deck = np.arange(128)
    marks = ((low[:, None] == deck) | (high[:, None] == deck)).astype(np.float32)
    pairs = np.zeros((HANDS + 256, HANDS), np.float32)
    pairs[0:HANDS] = marks @ marks.T == 0
    for copy in range(3):
        first = HANDS + 64 * copy
        pairs[first : first + 52] = marks.T[0:52]
        pairs[first + 52] = 0.5

    turn_cards = turn_cards.T
    packed, pairs = send(
        turn_cards,
        jnp.transpose(cum_turn, (0, 2, 1)),
        opp_init.T,
        strength,
        cum_river,
        jnp.asarray(pairs, jnp.bfloat16),
    )
    packed = packed.reshape(DEVICES, BLOCKS // 2, 2, 128)
    recv = lax.all_to_all(packed, AXES, split_axis=0, concat_axis=0, tiled=True)
    river, sums = boards(
        turn_cards,
        jnp.asarray(cards),
        recv.reshape(DEVICES * BLOCKS, 128),
        pairs,
    )
    back = lax.all_to_all(
        sums.reshape(DEVICES, 1, 128), AXES, split_axis=0, concat_axis=0, tiled=True
    )
    river = river.reshape(LOCAL, LINES, OWNED, DEVICES)
    river_value = jnp.transpose(river, (0, 1, 3, 2)).reshape(LOCAL, LINES, HANDS)
    return river_value, turns(back.reshape(DEVICES, 128)).T


def solution(mesh):
    placed = (
        P(AXES, None, None),
        P(AXES, None, None, None),
        P(AXES, None),
        P(),
        P(AXES, None),
    )
    return jax.shard_map(
        body,
        mesh=mesh,
        in_specs=placed,
        out_specs=(P(AXES, None, None), P(AXES, None)),
        check_vma=False,
    )
```
